256 devices in a mesh: pipe: 16 (over y, z_lo), expert: 16 (over x, z_hi, core).
Axes of the slice: x: 4, y: 4, z: 8 (z_hi: 2, z_lo: 4; z = z_hi * 4 + z_lo), core: 2. Of those that a mesh axis runs over, the one named last changes fastest.
Arguments:
- entering: bfloat16 [2, 512, 2048], P(None, 'expert'), may hold values from -6 to 6
- first_gain: float32 [16, 2048], P('pipe'), may hold values from 0.1 to 1.9
- first_gate: bfloat16 [16, 16, 2048, 384], P('pipe', 'expert'), may hold values from -0.125 to 0.125
- first_up: bfloat16 [16, 16, 2048, 384], P('pipe', 'expert'), may hold values from -0.125 to 0.125
- first_down: bfloat16 [16, 16, 384, 2048], P('pipe', 'expert'), may hold values from -0.3125 to 0.3125
- first_route: int32 [16, 2, 512, 1], P('pipe', None, 'expert'), may hold values from 0 to 15; in each aligned block of 32 rows (0 to 31, 32 to 63, ..., all dimensions but the last counted through in order) at most 4 rows name the same one
- first_share: float32 [16, 2, 512], P('pipe', None, 'expert'), may hold values from 0.2 to 1
- saved_inputs: bfloat16 [16, 2, 512, 2048], P('pipe', None, 'expert'), may hold values from -6 to 6
- cotangent: bfloat16 [2, 512, 2048], P(None, 'expert'), may hold values from -6 to 6
- second_gain: float32 [16, 2048], P('pipe'), may hold values from 0.1 to 1.9
- second_gate: bfloat16 [16, 16, 2048, 384], P('pipe', 'expert'), may hold values from -0.125 to 0.125
- second_up: bfloat16 [16, 16, 2048, 384], P('pipe', 'expert'), may hold values from -0.125 to 0.125
- second_down: bfloat16 [16, 16, 384, 2048], P('pipe', 'expert'), may hold values from -0.3125 to 0.3125
- second_route: int32 [16, 2, 512, 1], P('pipe', None, 'expert'), may hold values from 0 to 15; in each aligned block of 32 rows (0 to 31, 32 to 63, ..., all dimensions but the last counted through in order) at most 4 rows name the same one
- second_share: float32 [16, 2, 512], P('pipe', None, 'expert'), may hold values from 0.2 to 1
Outputs:
- forward_states: bfloat16 [16, 2, 512, 2048], P('pipe', None, 'expert')
- input_grads: bfloat16 [16, 2, 512, 2048], P('pipe', None, 'expert')
The draws below stay inside these ranges and needn't reach their ends.
Inputs may be any that keep to these rules, and one draw needn't show every extreme that they name: `first_route`: in each aligned block of 32 rows (the tokens of one device in one layer and micro-batch) no expert is named by more than 4 rows. `second_route`: in each aligned block of 32 rows (the tokens of one device in one layer and micro-batch) no expert is named by more than 4 rows.
All inputs are finite; a program needn't handle non-finite values.
Results may differ from the reference program's by a relative error of at most 0.035.
Values may be sent and summed in bfloat16 or wider, within the bound.
A program may use at most 64 MiB of HBM per device.

```python
import math
import jax
import jax.numpy as jnp
import numpy as np
from jax import lax

D = 2048
FFW = 384
TOK_DEV = 32
M = 2
TOP = 1
PIPE = 16
EXPERTS = 16
CAP = 4
ROWS_EXP = 64
TOKENS = 512
N_EXPERT = 16


def block_scale(own_key, extent, pieces, low, largest):
    def one(dim, shards_of):
        heights = jax.random.uniform(jax.random.fold_in(jax.random.fold_in(own_key, 6), dim), (shards_of,), jnp.float32, low / len(pieces), largest / len(pieces))
        return jnp.repeat(jnp.exp(heights), extent[dim] // shards_of).reshape((-1,) + (1,) * (len(extent) - dim - 1))

    loudness = one(*pieces[0])
    for cut in pieces[1:]:
        loudness = loudness * one(*cut)
    return loudness


def deal_out(stream_key, own, number, rows, number_of, top, reach, slope):
    sequence = jax.random.permutation(stream_key, number_of)
    heavy_load, usual = load_shares(number_of, rows * top, reach, slope, True), load_shares(number_of, rows * top, reach, slope, False)
    places = jnp.arange(number_of)

    def named(tallies, offset_by):
        used = int((tallies > 0).sum())
        fixed = max(1, used // 4)
        passed = fixed + (places - fixed + offset_by * (used - fixed)) % max(1, number_of - fixed)
        return jnp.zeros((number_of,), jnp.int32).at[sequence[jnp.where(places < fixed, places, passed)]].set(jnp.asarray(tallies, jnp.int32))

    tallies = jnp.where(number % 4 == 0, named(heavy_load, number // 4), named(usual, number - number // 4 - 1))
    mixed = jax.random.permutation(jax.random.fold_in(own, 3), number_of)
    donor, sink = mixed[0:number_of // 2 * 2:2], mixed[1:number_of // 2 * 2:2]
    slack = jnp.minimum(tallies[donor] - 1, reach - tallies[sink]) // 2
    slack = jnp.where((donor == sequence[0]) | (sink == sequence[0]) | (tallies[sink] == 0), 0, jnp.maximum(slack, 0))
    passed = jax.random.randint(jax.random.fold_in(own, 4), (number_of // 2,), 0, 1 << 20) % (slack + 1)
    tallies = tallies.at[donor].add(-passed).at[sink].add(passed)
    items = jnp.searchsorted(jnp.cumsum(tallies), jnp.arange(rows * top), side="right").astype(jnp.int32)
    listing = items.reshape(top, rows).T
    listing = listing[jax.random.permutation(jax.random.fold_in(own, 1), rows)]
    offset_by = jax.random.randint(jax.random.fold_in(own, 2), (rows, 1), 0, top)
    return jnp.take_along_axis(listing, (jnp.arange(top)[None, :] + offset_by) % top, axis=1)


def load_shares(count, total, bound, lean, full):
    portions = [(1 << 20) // math.isqrt(standing ** lean) + 1 for standing in range(1, count + 1)]
    largest = bound if full else min(bound, max(-(-total // count), total * portions[0] // sum(portions)))
    least = 1 if total - largest >= count - 1 else 0
    given, surplus = [largest] + [least] * (count - 1), total - largest - least * (count - 1)
    while surplus > 0:
        free = [i for i in range(1, count) if given[i] < largest] or [i for i in range(1, count) if given[i] < bound]
        mass, budget = sum([portions[i] for i in free]), surplus
        for i in free:
            addition = min(bound - given[i], max(1, budget * portions[i] // mass), surplus)
            given[i] = given[i] + addition
            surplus = surplus - addition
    return np.array(given)


def bell_draw(own_key, shape, scale, bound, shards=(), kind=jnp.bfloat16):
    gain = block_scale(own_key, shape, shards, -0.22, 0.18) if shards else 1.0
    values = jax.random.normal(own_key, shape, jnp.float32) * scale * gain
    return jnp.minimum(jnp.maximum(values, -bound), bound).astype(kind)


def setup_inputs(seed: int = 0) -> dict:
    splits = jax.random.split(jax.random.key(seed), 16)
    entering = bell_draw(splits[0], (M, TOKENS, D), 1.0, 6.0, ((1, 16),))
    first_gain = jnp.clip(1.0 + 0.18 * jax.random.normal(splits[1], (PIPE, D), jnp.float32), 0.1, 1.9)
    first_gate = bell_draw(splits[2], (PIPE, EXPERTS, D, FFW), D ** -0.5, 0.125, ((0, 16), (1, 16)))
    first_up = bell_draw(splits[3], (PIPE, EXPERTS, D, FFW), D ** -0.5, 0.125, ((0, 16), (1, 16)))
    first_down = bell_draw(splits[4], (PIPE, EXPERTS, FFW, D), FFW ** -0.5, 0.3125, ((0, 16), (1, 16)))
    first_route_keys = jax.random.split(jax.random.fold_in(splits[5], 1), PIPE * M * TOKENS // TOK_DEV)
    first_route_turns = jax.random.permutation(jax.random.fold_in(splits[5], 3), PIPE * M * TOKENS // TOK_DEV)
    first_route = jax.vmap(lambda own, number: deal_out(jax.random.fold_in(splits[5], 2), own, number, TOK_DEV, EXPERTS, TOP, CAP, 2))(first_route_keys, first_route_turns).reshape((PIPE, M, TOKENS, TOP))
    first_share = jnp.clip(0.2 + 0.8 * jax.random.uniform(splits[6], (PIPE, M, TOKENS), jnp.float32) ** block_scale(splits[6], (PIPE, M, TOKENS), ((0, 16), (2, 16)), -0.2, 0.2), 0.2, 1.0)
    saved_inputs = bell_draw(splits[7], (PIPE, M, TOKENS, D), 1.0, 6.0, ((0, 16), (2, 16)))
    cotangent = bell_draw(splits[8], (M, TOKENS, D), 1.0, 6.0, ((1, 16),))
    second_gain = jnp.clip(1.0 + 0.18 * jax.random.normal(splits[9], (PIPE, D), jnp.float32), 0.1, 1.9)
    second_gate = bell_draw(splits[10], (PIPE, EXPERTS, D, FFW), D ** -0.5, 0.125, ((0, 16), (1, 16)))
    second_up = bell_draw(splits[11], (PIPE, EXPERTS, D, FFW), D ** -0.5, 0.125, ((0, 16), (1, 16)))
    second_down = bell_draw(splits[12], (PIPE, EXPERTS, FFW, D), FFW ** -0.5, 0.3125, ((0, 16), (1, 16)))
    second_route_keys = jax.random.split(jax.random.fold_in(splits[13], 1), PIPE * M * TOKENS // TOK_DEV)
    second_route_turns = jax.random.permutation(jax.random.fold_in(splits[13], 3), PIPE * M * TOKENS // TOK_DEV)
    second_route = jax.vmap(lambda own, number: deal_out(jax.random.fold_in(splits[13], 2), own, number, TOK_DEV, EXPERTS, TOP, CAP, 2))(second_route_keys, second_route_turns).reshape((PIPE, M, TOKENS, TOP))
    second_share = jnp.clip(0.2 + 0.8 * jax.random.uniform(splits[14], (PIPE, M, TOKENS), jnp.float32) ** block_scale(splits[14], (PIPE, M, TOKENS), ((0, 16), (2, 16)), -0.2, 0.2), 0.2, 1.0)
    return dict(entering=entering, first_gain=first_gain, first_gate=first_gate, first_up=first_up, first_down=first_down, first_route=first_route, first_share=first_share, saved_inputs=saved_inputs, cotangent=cotangent, second_gain=second_gain, second_gate=second_gate, second_up=second_up, second_down=second_down, second_route=second_route, second_share=second_share)


EPSILON = 1e-06

def rms_scaled(values, gain_vector):
    squares = lax.optimization_barrier(jnp.mean(values * values, axis=-1, keepdims=True))
    return values * lax.rsqrt(squares + EPSILON) * gain_vector

def row_index(route_ids):
    blocks = route_ids.reshape(N_EXPERT, TOK_DEV).astype(jnp.int32)
    member = (blocks[:, :, None] == jnp.arange(EXPERTS, dtype=jnp.int32)[None, None, :]).astype(jnp.int32)
    before = jnp.cumsum(member, axis=1) - member
    slots = lax.optimization_barrier(jnp.sum(member * before, axis=-1))
    source = jnp.arange(N_EXPERT, dtype=jnp.int32)[:, None]
    target = blocks * ROWS_EXP + source * CAP + slots
    return target.reshape(-1).astype(jnp.int32)

def scatter_rows(values, target):
    empty_rows = jnp.zeros((EXPERTS * ROWS_EXP, D), jnp.bfloat16)
    return empty_rows.at[target].set(values).reshape(EXPERTS, ROWS_EXP, D)

def expert_forward(operands):
    expert_rows, gate_w, up_w, down_w = operands
    pre_gate = jnp.dot(expert_rows, gate_w, preferred_element_type=jnp.float32)
    pre_up = jnp.dot(expert_rows, up_w, preferred_element_type=jnp.float32)
    hidden = (jax.nn.silu(pre_gate) * pre_up).astype(jnp.bfloat16)
    return jnp.dot(hidden, down_w, preferred_element_type=jnp.float32).astype(jnp.bfloat16)

def expert_backward(operands):
    expert_rows, sent_rows, gate_w, up_w, down_w = operands
    back_gate = jnp.dot(expert_rows, gate_w, preferred_element_type=jnp.float32)
    back_up = jnp.dot(expert_rows, up_w, preferred_element_type=jnp.float32)
    d_hidden = lax.dot_general(sent_rows, down_w, (((1,), (1,)), ((), ())), preferred_element_type=jnp.float32)
    sigmoid_gate = jax.nn.sigmoid(back_gate)
    d_gate = (d_hidden * back_up * sigmoid_gate * (1.0 + back_gate * (1.0 - sigmoid_gate))).astype(jnp.bfloat16)
    d_up = (d_hidden * back_gate * sigmoid_gate).astype(jnp.bfloat16)
    first_term = lax.dot_general(d_gate, gate_w, (((1,), (1,)), ((), ())), preferred_element_type=jnp.float32)
    second_term = lax.dot_general(d_up, up_w, (((1,), (1,)), ((), ())), preferred_element_type=jnp.float32)
    return (first_term + second_term).astype(jnp.bfloat16)

def forward_layer(states, gain_vector, gate_w, up_w, down_w, route_ids, share_row):
    target = row_index(route_ids)
    normed = rms_scaled(states.astype(jnp.float32), gain_vector).astype(jnp.bfloat16)
    outputs = lax.map(expert_forward, (scatter_rows(normed, target), gate_w, up_w, down_w))
    combined = outputs.reshape(-1, D)[target].astype(jnp.float32)
    return (states.astype(jnp.float32) + share_row[:, None] * combined).astype(jnp.bfloat16)

def backward_layer(saved_rows, upstream, gain_vector, gate_w, up_w, down_w, route_ids, share_row):
    target = row_index(route_ids)
    normed, pullback = jax.vjp(lambda values: rms_scaled(values, gain_vector), saved_rows.astype(jnp.float32))
    normed = normed.astype(jnp.bfloat16)
    sent_rows = (share_row[:, None] * upstream.astype(jnp.float32)).astype(jnp.bfloat16)
    d_rows = lax.map(expert_backward, (scatter_rows(normed, target), scatter_rows(sent_rows, target), gate_w, up_w, down_w))
    d_normed = d_rows.reshape(-1, D)[target].astype(jnp.float32)
    return (upstream.astype(jnp.float32) + pullback(d_normed)[0]).astype(jnp.bfloat16)

def reference(entering, first_gain, first_gate, first_up, first_down, first_route, first_share, saved_inputs, cotangent, second_gain, second_gate, second_up, second_down, second_route, second_share):
    forward_list = []
    backward_list = []
    for micro_index in range(M):
        states = entering[micro_index]
        layer_states = []
        for layer_index in range(PIPE):
            states = forward_layer(states, first_gain[layer_index], first_gate[layer_index], first_up[layer_index], first_down[layer_index], first_route[layer_index, micro_index, :, 0], first_share[layer_index, micro_index])
            layer_states.append(states)
        forward_list.append(jnp.stack(layer_states))
        upstream = cotangent[micro_index]
        layer_grads = []
        for layer_index in range(PIPE):
            upstream = backward_layer(saved_inputs[layer_index, micro_index], upstream, second_gain[layer_index], second_gate[layer_index], second_up[layer_index], second_down[layer_index], second_route[layer_index, micro_index, :, 0], second_share[layer_index, micro_index])
            layer_grads.append(upstream)
        backward_list.append(jnp.stack(layer_grads))
    return (jnp.stack(forward_list, axis=1), jnp.stack(backward_list, axis=1))
```

```python
import functools

import jax
import jax.numpy as jnp
from jax import lax
from jax.experimental import pallas as pl
from jax.experimental.pallas import tpu as pltpu
from jax.sharding import PartitionSpec as P

EPSILON = 1e-06
MESH = pl.DeviceIdType.MESH
F32 = jnp.float32
BF16 = jnp.bfloat16
ROWS = 16


def iota(shape, dim):
    return lax.broadcasted_iota(jnp.int32, shape, dim)


def dot(a, b):
    return jnp.dot(a, b, preferred_element_type=F32)


def dot_nt(a, b):
    return lax.dot_general(a, b, (((1,), (1,)), ((), ())), preferred_element_type=F32)


def dot_tn(a, b):
    return lax.dot_general(a, b, (((0,), (0,)), ((), ())), preferred_element_type=F32)


def kernel(
    sizes,
    entering,
    cotangent,
    saved,
    gain_f,
    gain_b,
    route_f,
    route_b,
    share_f,
    share_b,
    gate_f,
    up_f,
    down_f,
    gate_b,
    up_b,
    down_b,
    out_f,
    out_b,
    gu_f,
    dn_f,
    gu_b,
    dn_b,
    ein,
    eout,
    rin,
    rout,
    disp,
    sdisp,
    sin,
    msend,
    mrecv,
    mflat,
    csend,
    crecv,
    perm,
    permt,
    rmat,
    aexp,
    vrows,
    fact1,
    fact2,
    rsaved,
    w_sem,
    ein_sem,
    rin_sem,
    sin_sem,
    m_sem,
    c_sem,
    eout_sem,
    rout_sem,
    disp_sem,
    sdisp_sem,
    msend_sem,
    csend_sem,
):
    stages, group, micro, tokens, width, hidden_width, cap = sizes
    parts = ROWS // cap
    wide = width // parts
    rows = group * cap
    total = group * ROWS
    chains = 2 * micro
    stage = lax.axis_index("pipe")
    me = lax.axis_index("expert")
    first = stage == 0
    last = stage == stages - 1

    weights = [
        (gate_f.at[0, 0], gu_f.at[:, 0:hidden_width]),
        (up_f.at[0, 0], gu_f.at[:, hidden_width : 2 * hidden_width]),
        (down_f.at[0, 0], dn_f),
        (gate_b.at[0, 0], gu_b.at[:, 0:hidden_width]),
        (up_b.at[0, 0], gu_b.at[:, hidden_width : 2 * hidden_width]),
        (down_b.at[0, 0], dn_b),
    ]
    loads = [pltpu.make_async_copy(s, d, w_sem.at[i]) for i, (s, d) in enumerate(weights)]
    for load in (loads[3], loads[4], loads[0], loads[1], loads[2], loads[5]):
        load.start()

    barrier = pltpu.get_barrier_semaphore()

    def greet(pipe, peer):
        pl.semaphore_signal(barrier, inc=1, device_id=(pipe, peer), device_id_type=MESH)

    def greet_group(i, carry):
        greet(stage, lax.rem(me + i, group))
        return carry

    lax.fori_loop(1, group, greet_group, 0)

    @pl.when(stage > 0)
    def _():
        def greet_before(i, carry):
            greet(stage - 1, lax.rem(me + i, group))
            return carry

        lax.fori_loop(0, group, greet_before, 0)

    @pl.when(stage < stages - 1)
    def _():
        greet(stage + 1, me)

    def column_to_row(column):
        eye = iota((tokens, tokens), 0) == iota((tokens, tokens), 1)
        return jnp.sum(jnp.where(eye, column, 0.0), axis=0, keepdims=True)

    def row_to_column(row):
        eye = iota((tokens, tokens), 0) == iota((tokens, tokens), 1)
        return jnp.sum(jnp.where(eye, row, 0.0), axis=1, keepdims=True)

    def code_of(route_column):
        member = (iota((tokens, 128), 1) == route_column).astype(BF16)
        same = dot_nt(member, member)
        before = iota((tokens, tokens), 1) < iota((tokens, tokens), 0)
        slot = jnp.sum(jnp.where(before, same, 0.0), axis=1, keepdims=True)
        return route_column.astype(F32) * ROWS + slot

    def expanded(code):
        column = jnp.concatenate([code + q * cap for q in range(parts)], axis=0)
        return (iota((parts * tokens, total), 1).astype(F32) == column).astype(BF16)

    codes = []
    for micro_index in range(micro):
        for route in (route_f, route_b):
            codes.append(code_of(route[0, micro_index]))
    for c in range(chains):
        aexp[c] = expanded(codes[c])

    def chunk_row(index):
        return lax.rem(index, rows) // cap * ROWS + index // rows * cap + lax.rem(index, cap)

    perm[...] = (iota((total, total), 1) == chunk_row(iota((total, total), 0))).astype(BF16)
    permt[...] = (iota((total, total), 0) == chunk_row(iota((total, total), 1))).astype(BF16)

    def stacked(values):
        return jnp.concatenate([values[:, q * wide : (q + 1) * wide] for q in range(parts)], axis=0)

    def scatter(c, values):
        return dot_tn(aexp[c], stacked(values)).astype(BF16).reshape(group, ROWS, wide)

    def send_chunks(source, target, pipe, send_sem, recv_sem, begin):
        def send(i, carry):
            peer = lax.rem(me + i, group)
            pltpu.make_async_remote_copy(
                src_ref=source.at[peer],
                dst_ref=target.at[me],
                send_sem=send_sem,
                recv_sem=recv_sem,
                device_id=(pipe, peer),
                device_id_type=MESH,
            ).start()
            return carry

        lax.fori_loop(begin, group, send, 0)

    def send_group(source, target, send_sem, recv_sem):
        send_chunks(source, target, stage, send_sem, recv_sem, 1)
        pltpu.make_async_copy(source.at[me], target.at[me], recv_sem).start()

    def wait_bytes(ref, sem):
        pltpu.make_async_copy(ref, ref, sem).wait()

    greeted = group - 1 + jnp.where(last, 0, group) + jnp.where(first, 0, 1)
    pl.semaphore_wait(barrier, greeted)

    @pl.when(first)
    def _():
        for c in range(chains):
            source = entering if c % 2 == 0 else cotangent
            disp[c] = scatter(c, source[c // 2])
            send_group(disp.at[c], ein.at[c], disp_sem.at[c], ein_sem.at[c])

    for direction, share in ((0, share_f), (1, share_b)):
        column = jnp.zeros((rows * micro, 1), F32)
        for micro_index in range(micro):
            code_row = column_to_row(codes[2 * micro_index + direction])
            index = iota((rows * micro, tokens), 0)
            row_code = index // (cap * micro) * ROWS + lax.rem(index, cap * micro) // micro
            hit = jnp.logical_and(
                row_code.astype(F32) == code_row, lax.rem(index, micro) == micro_index
            )
            share_row = share[0, micro_index : micro_index + 1]
            column = column + jnp.sum(jnp.where(hit, share_row, 0.0), axis=1, keepdims=True)
        msend[:, :, direction * 64 : direction * 64 + 64] = jnp.broadcast_to(
            column, (rows * micro, 64)
        ).reshape(group, cap * micro, 64)
    send_group(msend, mrecv, msend_sem, m_sem)

    for micro_index in range(micro):
        sdisp[micro_index] = scatter(2 * micro_index + 1, saved[0, micro_index])
        send_group(
            sdisp.at[micro_index], sin.at[micro_index], sdisp_sem.at[micro_index], sin_sem.at[micro_index]
        )

    lane = iota((tokens, 128), 1)
    packed = jnp.zeros((tokens, 128), F32)
    for c in range(chains):
        packed = packed + jnp.where(lane == c, codes[c], 0.0)
    csend[...] = packed

    def code_copy():
        return pltpu.make_async_remote_copy(
            src_ref=csend,
            dst_ref=crecv,
            send_sem=csend_sem,
            recv_sem=c_sem,
            device_id=(lax.rem(stage + stages - 1, stages), me),
            device_id_type=MESH,
        )

    @pl.when(stage > 0)
    def _():
        code_copy().start()

    def arrange(chunks):
        return dot(perm[...], chunks.reshape(total, wide))

    def part(values, q):
        return values[q * rows : (q + 1) * rows]

    def gain_part(gain, q):
        return gain[:, q * wide : (q + 1) * wide]

    def row_sum(values, weigh):
        result = jnp.zeros((rows, 1), F32)
        for q in range(parts):
            result = result + jnp.sum(weigh(q, part(values, q)), axis=1, keepdims=True)
        return result

    def inverse_scale(values):
        squares = row_sum(values, lambda q, v: v * v) * (1.0 / width)
        return lax.rsqrt(squares + EPSILON)

    def normed(values, inverse, gain):
        return jnp.concatenate(
            [(part(values, q) * inverse * gain_part(gain, q)).astype(BF16) for q in range(parts)],
            axis=1,
        )

    def share_of(micro_index, direction):
        lanes = mflat[pl.ds(micro_index, rows, stride=micro), :]
        return lanes[:, direction * 64 : direction * 64 + 1]

    def finish(c, values):
        eout[c] = dot(permt[...], values).astype(BF16).reshape(group, ROWS, wide)
        send_group(eout.at[c], rin.at[c], eout_sem.at[c], rin_sem.at[c])

    def expert_forward(micro_index):
        c = 2 * micro_index
        wait_bytes(ein.at[c], ein_sem.at[c])
        x = arrange(ein[c])
        gain = gain_f[...]
        pre = dot(normed(x, inverse_scale(x), gain), gu_f[...])
        pre_gate, pre_up = pre[:, :hidden_width], pre[:, hidden_width:]
        hidden = (pre_gate / (1.0 + jnp.exp(-pre_gate)) * pre_up).astype(BF16)
        out = dot(hidden, dn_f[...]).astype(BF16).astype(F32)
        share = share_of(micro_index, 0)
        finish(
            c,
            jnp.concatenate(
                [
                    (part(x, q) + share * out[:, q * wide : (q + 1) * wide]).astype(BF16)
                    for q in range(parts)
                ],
                axis=0,
            ),
        )

    def prepare_backward(micro_index):
        wait_bytes(sin.at[micro_index], sin_sem.at[micro_index])
        v = arrange(sin[micro_index])
        vrows[micro_index] = v.astype(BF16)
        inverse = inverse_scale(v)
        rsaved[micro_index] = jnp.broadcast_to(inverse, (rows, 128))
        back = dot(normed(v, inverse, gain_b[...]), gu_b[...])
        back_gate, back_up = back[:, :hidden_width], back[:, hidden_width:]
        s = 1.0 / (1.0 + jnp.exp(-back_gate))
        fact1[micro_index] = back_up * s * (1.0 + back_gate * (1.0 - s))
        fact2[micro_index] = back_gate * s

    def expert_backward(micro_index):
        c = 2 * micro_index + 1
        wait_bytes(ein.at[c], ein_sem.at[c])
        dy = arrange(ein[c])
        share = share_of(micro_index, 1)
        sent = jnp.concatenate(
            [(share * part(dy, q)).astype(BF16) for q in range(parts)], axis=1
        )
        d_hidden = dot_nt(sent, dn_b[...])
        both = jnp.concatenate(
            [
                (d_hidden * fact1[micro_index]).astype(BF16),
                (d_hidden * fact2[micro_index]).astype(BF16),
            ],
            axis=1,
        )
        d_rows = dot_nt(both, gu_b[...]).astype(BF16).astype(F32)
        inverse = rsaved[micro_index][:, 0:1]
        gain = gain_b[...]
        scaled = [d_rows[:, q * wide : (q + 1) * wide] * gain_part(gain, q) for q in range(parts)]
        v = [vrows[micro_index, q * rows : (q + 1) * rows].astype(F32) for q in range(parts)]
        inner = jnp.zeros((rows, 1), F32)
        for q in range(parts):
            inner = inner + jnp.sum(scaled[q] * v[q], axis=1, keepdims=True)
        back = inner * (1.0 / width) * inverse * inverse * inverse
        finish(
            c,
            jnp.concatenate(
                [
                    (part(dy, q) + (scaled[q] * inverse - v[q] * back)).astype(BF16)
                    for q in range(parts)
                ],
                axis=0,
            ),
        )

    def relay(c):
        wait_bytes(rin.at[c], rin_sem.at[c])

        @pl.when(stage < stages - 1)
        def _():
            moved = dot(rmat[c], rin[c].reshape(total, wide))
            rout[c] = moved.astype(BF16).reshape(group, ROWS, wide)
            send_chunks(rout.at[c], ein.at[c], stage + 1, rout_sem.at[c], ein_sem.at[c], 0)

        kept = dot(aexp[c], rin[c].reshape(total, wide)).astype(BF16)
        out = out_f if c % 2 == 0 else out_b
        for q in range(parts):
            out[0, c // 2, :, q * wide : (q + 1) * wide] = kept[q * tokens : (q + 1) * tokens]

    wait_bytes(mrecv, m_sem)
    mflat[...] = mrecv[...].reshape(rows * micro, 128)
    loads[3].wait()
    loads[4].wait()
    for micro_index in range(micro):
        prepare_backward(micro_index)

    @pl.when(stage < stages - 1)
    def _():
        code_copy().wait_recv()
        for c in range(chains):
            rmat[c] = dot_tn(expanded(crecv[:, c : c + 1]), aexp[c]).astype(BF16)

    for i in (0, 1, 2, 5):
        loads[i].wait()

    expert_forward(0)
    expert_backward(0)
    expert_forward(1)
    relay(0)
    expert_backward(1)
    relay(1)
    relay(2)
    relay(3)

    @pl.when(stage > 0)
    def _():
        code_copy().wait_send()

    wait_bytes(msend.at[pl.ds(0, group - 1)], msend_sem)
    for micro_index in range(micro):
        wait_bytes(sdisp.at[micro_index, pl.ds(0, group - 1)], sdisp_sem.at[micro_index])
    for c in range(chains):
        wait_bytes(eout.at[c, pl.ds(0, group - 1)], eout_sem.at[c])

    @pl.when(first)
    def _():
        for c in range(chains):
            wait_bytes(disp.at[c, pl.ds(0, group - 1)], disp_sem.at[c])

    @pl.when(stage < stages - 1)
    def _():
        for c in range(chains):
            wait_bytes(rout.at[c], rout_sem.at[c])


def solution(mesh):
    stages, group = mesh.shape["pipe"], mesh.shape["expert"]

    def local(
        entering,
        first_gain,
        first_gate,
        first_up,
        first_down,
        first_route,
        first_share,
        saved_inputs,
        cotangent,
        second_gain,
        second_gate,
        second_up,
        second_down,
        second_route,
        second_share,
    ):
        micro, tokens, width = entering.shape
        hidden_width = first_gate.shape[-1]
        cap = 2 * tokens // group
        parts = ROWS // cap
        wide = width // parts
        rows, total, chains = group * cap, group * ROWS, 2 * micro
        vmem = pl.BlockSpec(memory_space=pltpu.VMEM)
        anywhere = pl.BlockSpec(memory_space=pl.ANY)
        dma = pltpu.SemaphoreType.DMA
        chunks = lambda count: pltpu.VMEM((count, group, ROWS, wide), BF16)
        state = jax.ShapeDtypeStruct((1, micro, tokens, width), BF16)
        return pl.pallas_call(
            functools.partial(
                kernel, (stages, group, micro, tokens, width, hidden_width, cap)
            ),
            out_shape=(state, state),
            in_specs=[vmem] * 9 + [anywhere] * 6,
            out_specs=(vmem, vmem),
            scratch_shapes=[
                pltpu.VMEM((width, 2 * hidden_width), BF16),
                pltpu.VMEM((hidden_width, width), BF16),
                pltpu.VMEM((width, 2 * hidden_width), BF16),
                pltpu.VMEM((hidden_width, width), BF16),
                chunks(chains),
                chunks(chains),
                chunks(chains),
                chunks(chains),
                chunks(chains),
                chunks(micro),
                chunks(micro),
                pltpu.VMEM((group, cap * micro, 128), F32),
                pltpu.VMEM((group, cap * micro, 128), F32),
                pltpu.VMEM((rows * micro, 128), F32),
                pltpu.VMEM((tokens, 128), F32),
                pltpu.VMEM((tokens, 128), F32),
                pltpu.VMEM((total, total), BF16),
                pltpu.VMEM((total, total), BF16),
                pltpu.VMEM((chains, total, total), BF16),
                pltpu.VMEM((chains, parts * tokens, total), BF16),
                pltpu.VMEM((micro, total, wide), BF16),
                pltpu.VMEM((micro, rows, hidden_width), F32),
                pltpu.VMEM((micro, rows, hidden_width), F32),
                pltpu.VMEM((micro, rows, 128), F32),
                dma((6,)),
                dma((chains,)),
                dma((chains,)),
                dma((micro,)),
                dma,
                dma,
                dma((chains,)),
                dma((chains,)),
                dma((chains,)),
                dma((micro,)),
                dma,
                dma,
            ],
            compiler_params=pltpu.CompilerParams(
                collective_id=0, has_side_effects=True, vmem_limit_bytes=48 * 1024 * 1024
            ),
        )(
            entering,
            cotangent,
            saved_inputs,
            first_gain,
            second_gain,
            first_route,
            second_route,
            first_share,
            second_share,
            first_gate,
            first_up,
            first_down,
            second_gate,
            second_up,
            second_down,
        )

    return jax.shard_map(
        local,
        mesh=mesh,
        in_specs=(
            P(None, "expert", None),
            P("pipe", None),
            P("pipe", "expert", None, None),
            P("pipe", "expert", None, None),
            P("pipe", "expert", None, None),
            P("pipe", None, "expert", None),
            P("pipe", None, "expert"),
            P("pipe", None, "expert", None),
            P(None, "expert", None),
            P("pipe", None),
            P("pipe", "expert", None, None),
            P("pipe", "expert", None, None),
            P("pipe", "expert", None, None),
            P("pipe", None, "expert", None),
            P("pipe", None, "expert"),
        ),
        out_specs=(P("pipe", None, "expert", None), P("pipe", None, "expert", None)),
        check_vma=False,
    )
```

```python
import functools

import jax
import jax.numpy as jnp
from jax import lax
from jax.experimental import pallas as pl
from jax.experimental.pallas import tpu as pltpu
from jax.sharding import PartitionSpec as P

EPSILON = 1e-06
MESH = pl.DeviceIdType.MESH
F32 = jnp.float32
BF16 = jnp.bfloat16
ROWS = 16
NEAR = 4


def shift_of(block):
    return jnp.where(block % 4 == 1, NEAR, 0) - jnp.where(block % 4 == 3, NEAR, 0)


def relay_of(stage, block, stages):
    return lax.rem(stage + shift_of(block) + stages, stages)


def relayed_by(place, block, stages):
    return lax.rem(place - shift_of(block) + stages, stages)


def iota(shape, dim):
    return lax.broadcasted_iota(jnp.int32, shape, dim)


def dot(a, b):
    return jnp.dot(a, b, preferred_element_type=F32)


def dot_nt(a, b):
    return lax.dot_general(a, b, (((1,), (1,)), ((), ())), preferred_element_type=F32)


def dot_tn(a, b):
    return lax.dot_general(a, b, (((0,), (0,)), ((), ())), preferred_element_type=F32)


def kernel(
    sizes,
    entering,
    cotangent,
    saved,
    gain_f,
    gain_b,
    route_f,
    route_b,
    share_f,
    share_b,
    gate_f,
    up_f,
    down_f,
    gate_b,
    up_b,
    down_b,
    out_f,
    out_b,
    gu_f,
    dn_f,
    gu_b,
    dn_b,
    ein,
    eout,
    rin,
    rout,
    disp,
    sdisp,
    sin,
    msend,
    mrecv,
    mflat,
    shares,
    csend,
    crecv,
    cnext,
    perm,
    permt,
    rmat,
    aexp,
    vrows,
    fact1,
    fact2,
    rsaved,
    kept,
    w_sem,
    ein_sem,
    rin_sem,
    sin_sem,
    m_sem,
    c_sem,
    cnext_sem,
    out_sem,
    eout_sem,
    rout_sem,
    disp_sem,
    sdisp_sem,
    msend_sem,
    csend_sem,
    cnsend_sem,
    kept_sem,
):
    stages, group, micro, tokens, width, hidden_width, cap = sizes
    parts = ROWS // cap
    wide = width // parts
    rows = group * cap
    total = group * ROWS
    chains = 2 * micro
    stage = lax.axis_index("pipe")
    me = lax.axis_index("expert")
    first = stage == 0
    host = relay_of(stage, me, stages)
    source_stage = relayed_by(stage, me, stages)
    has_next = source_stage < stages - 1
    at_home = host == stage

    weights = [
        (gate_f.at[0, 0], gu_f.at[:, 0:hidden_width]),
        (up_f.at[0, 0], gu_f.at[:, hidden_width : 2 * hidden_width]),
        (down_f.at[0, 0], dn_f),
        (gate_b.at[0, 0], gu_b.at[:, 0:hidden_width]),
        (up_b.at[0, 0], gu_b.at[:, hidden_width : 2 * hidden_width]),
        (down_b.at[0, 0], dn_b),
    ]
    loads = [pltpu.make_async_copy(s, d, w_sem.at[i]) for i, (s, d) in enumerate(weights)]
    for load in (loads[3], loads[4], loads[0], loads[1], loads[2], loads[5]):
        load.start()

    barrier = pltpu.get_barrier_semaphore()

    def greet(pipe, peer):
        pl.semaphore_signal(barrier, inc=1, device_id=(pipe, peer), device_id_type=MESH)

    def greet_group(i, carry):
        greet(stage, lax.rem(me + i, group))
        return carry

    lax.fori_loop(1, group, greet_group, 0)

    @pl.when(jnp.logical_not(at_home))
    def _():
        def greet_source(i, carry):
            greet(source_stage, lax.rem(me + i, group))
            return carry

        lax.fori_loop(0, group, greet_source, 0)
        greet(host, me)

    @pl.when(stage > 0)
    def _():
        def greet_before(i, carry):
            peer = lax.rem(me + i, group)
            greet(relay_of(stage - 1, peer, stages), peer)
            return carry

        lax.fori_loop(0, group, greet_before, 0)

    @pl.when(has_next)
    def _():
        greet(source_stage + 1, me)

    def column_to_row(column):
        eye = iota((tokens, tokens), 0) == iota((tokens, tokens), 1)
        return jnp.sum(jnp.where(eye, column, 0.0), axis=0, keepdims=True)

    def row_to_column(row):
        eye = iota((tokens, tokens), 0) == iota((tokens, tokens), 1)
        return jnp.sum(jnp.where(eye, row, 0.0), axis=1, keepdims=True)

    def code_of(route_column):
        member = (iota((tokens, 128), 1) == route_column).astype(BF16)
        same = dot_nt(member, member)
        before = iota((tokens, tokens), 1) < iota((tokens, tokens), 0)
        slot = jnp.sum(jnp.where(before, same, 0.0), axis=1, keepdims=True)
        return route_column.astype(F32) * ROWS + slot

    def expanded(code):
        column = jnp.concatenate([code + q * cap for q in range(parts)], axis=0)
        return (iota((parts * tokens, total), 1).astype(F32) == column).astype(BF16)

    codes = []
    for micro_index in range(micro):
        for route in (route_f, route_b):
            codes.append(code_of(route[0, micro_index]))
    def chunk_row(index):
        return lax.rem(index, rows) // cap * ROWS + index // rows * cap + lax.rem(index, cap)

    perm[...] = (iota((total, total), 1) == chunk_row(iota((total, total), 0))).astype(BF16)
    permt[...] = (iota((total, total), 0) == chunk_row(iota((total, total), 1))).astype(BF16)

    def stacked(values):
        return jnp.concatenate([values[:, q * wide : (q + 1) * wide] for q in range(parts)], axis=0)

    def scatter(table, values):
        return dot_tn(table, stacked(values)).astype(BF16).reshape(group, ROWS, wide)

    def send_chunks(source, target, pipe_of, far, count, send_sem, recv_sem):
        def send(i, carry):
            across, j = i // 8, i % 8 // 2
            step_x = jnp.where(j < 2, 2 + j, 3 - j)
            peer = (
                (me // 4 + step_x) % 4 * 4 + (me % 4 // 2 + far + across) % 2 * 2 + (me + 1 + i) % 2
            )
            pltpu.make_async_remote_copy(
                src_ref=source.at[peer],
                dst_ref=target.at[me],
                send_sem=send_sem,
                recv_sem=recv_sem,
                device_id=(pipe_of(peer), peer),
                device_id_type=MESH,
            ).start()
            return carry

        lax.fori_loop(0, count, send, 0)

    def send_group(source, target, send_sem, recv_sem):
        send_chunks(source, target, lambda peer: stage, 1, group - 1, send_sem, recv_sem)
        pltpu.make_async_copy(source.at[me], target.at[me], recv_sem).start()

    def wait_bytes(ref, sem):
        pltpu.make_async_copy(ref, ref, sem).wait()

    greeted = (
        group - 1
        + group // 2
        + jnp.where(has_next, group, 0)
        + jnp.where(first, 0, 1)
        + jnp.where(at_home, 0, 1)
    )
    pl.semaphore_wait(barrier, greeted)

    def deal(micro_index):
        for c in (2 * micro_index, 2 * micro_index + 1):
            source = entering if c % 2 == 0 else cotangent
            disp[c] = scatter(expanded(codes[c]), source[micro_index])
            send_group(disp.at[c], ein.at[c], disp_sem.at[c], ein_sem.at[c])

    @pl.when(first)
    def _():
        deal(0)

    for direction, share in ((0, share_f), (1, share_b)):
        column = jnp.zeros((rows * micro, 1), F32)
        for micro_index in range(micro):
            code_row = column_to_row(codes[2 * micro_index + direction])
            index = iota((rows * micro, tokens), 0)
            row_code = index // (cap * micro) * ROWS + lax.rem(index, cap * micro) // micro
            hit = jnp.logical_and(
                row_code.astype(F32) == code_row, lax.rem(index, micro) == micro_index
            )
            share_row = share[0, micro_index : micro_index + 1]
            column = column + jnp.sum(jnp.where(hit, share_row, 0.0), axis=1, keepdims=True)
        msend[:, :, direction * 64 : direction * 64 + 64] = jnp.broadcast_to(
            column, (rows * micro, 64)
        ).reshape(group, cap * micro, 64)
    send_group(msend, mrecv, msend_sem, m_sem)

    for micro_index in range(micro):
        sdisp[micro_index] = scatter(expanded(codes[2 * micro_index + 1]), saved[0, micro_index])
        send_group(
            sdisp.at[micro_index], sin.at[micro_index], sdisp_sem.at[micro_index], sin_sem.at[micro_index]
        )

    lane = iota((tokens, 128), 1)
    packed = jnp.zeros((tokens, 128), F32)
    for c in range(chains):
        packed = packed + jnp.where(lane == c, codes[c], 0.0)
    csend[...] = packed

    def code_copy(target, send_sem, recv_sem, pipe):
        return pltpu.make_async_remote_copy(
            src_ref=csend,
            dst_ref=target,
            send_sem=send_sem,
            recv_sem=recv_sem,
            device_id=(pipe, me),
            device_id_type=MESH,
        )

    @pl.when(at_home)
    def _():
        pltpu.make_async_copy(csend, crecv, c_sem).start()

    @pl.when(jnp.logical_not(at_home))
    def _():
        code_copy(crecv, csend_sem, c_sem, host).start()

    @pl.when(stage > 0)
    def _():
        code_copy(cnext, cnsend_sem, cnext_sem, relay_of(stage - 1, me, stages)).start()

    def arrange(chunks):
        return dot(perm[...], chunks.reshape(total, wide))

    def part(values, q):
        return values[q * rows : (q + 1) * rows]

    def gain_part(gain, q):
        return gain[:, q * wide : (q + 1) * wide]

    def row_sum(values, weigh):
        result = jnp.zeros((rows, 1), F32)
        for q in range(parts):
            result = result + jnp.sum(weigh(q, part(values, q)), axis=1, keepdims=True)
        return result

    def inverse_scale(values):
        squares = row_sum(values, lambda q, v: v * v) * (1.0 / width)
        return lax.rsqrt(squares + EPSILON)

    def normed(values, inverse, gain):
        return jnp.concatenate(
            [(part(values, q) * inverse * gain_part(gain, q)).astype(BF16) for q in range(parts)],
            axis=1,
        )

    def finish(c, values):
        eout[c] = dot(permt[...], values).astype(BF16).reshape(group, ROWS, wide)
        send_chunks(
            eout.at[c],
            rin.at[c],
            lambda peer: relay_of(stage, peer, stages),
            1,
            group - 1,
            eout_sem.at[c],
            rin_sem.at[c],
        )

        @pl.when(at_home)
        def _():
            pltpu.make_async_copy(eout.at[c, me], rin.at[c, me], rin_sem.at[c]).start()

        @pl.when(jnp.logical_not(at_home))
        def _():
            pltpu.make_async_remote_copy(
                src_ref=eout.at[c, me],
                dst_ref=rin.at[c, me],
                send_sem=eout_sem.at[c],
                recv_sem=rin_sem.at[c],
                device_id=(host, me),
                device_id_type=MESH,
            ).start()

    def expert_forward(micro_index):
        c = 2 * micro_index
        wait_bytes(ein.at[c], ein_sem.at[c])
        x = arrange(ein[c])
        gain = gain_f[...]
        pre = dot(normed(x, inverse_scale(x), gain), gu_f[...])
        pre_gate, pre_up = pre[:, :hidden_width], pre[:, hidden_width:]
        hidden = (pre_gate / (1.0 + jnp.exp(-pre_gate)) * pre_up).astype(BF16)
        out = dot(hidden, dn_f[...]).astype(BF16).astype(F32)
        share = shares[c][:, 0:1]
        finish(
            c,
            jnp.concatenate(
                [
                    (part(x, q) + share * out[:, q * wide : (q + 1) * wide]).astype(BF16)
                    for q in range(parts)
                ],
                axis=0,
            ),
        )

    def prepare_backward(micro_index):
        wait_bytes(sin.at[micro_index], sin_sem.at[micro_index])
        v = arrange(sin[micro_index])
        vrows[micro_index] = v.astype(BF16)
        inverse = inverse_scale(v)
        rsaved[micro_index] = jnp.broadcast_to(inverse, (rows, 128))
        back = dot(normed(v, inverse, gain_b[...]), gu_b[...])
        back_gate, back_up = back[:, :hidden_width], back[:, hidden_width:]
        s = 1.0 / (1.0 + jnp.exp(-back_gate))
        fact1[micro_index] = back_up * s * (1.0 + back_gate * (1.0 - s))
        fact2[micro_index] = back_gate * s

    def expert_backward(micro_index):
        c = 2 * micro_index + 1
        wait_bytes(ein.at[c], ein_sem.at[c])
        dy = arrange(ein[c])
        share = shares[c][:, 0:1]
        sent = jnp.concatenate(
            [(share * part(dy, q)).astype(BF16) for q in range(parts)], axis=1
        )
        d_hidden = dot_nt(sent, dn_b[...])
        both = jnp.concatenate(
            [
                (d_hidden * fact1[micro_index]).astype(BF16),
                (d_hidden * fact2[micro_index]).astype(BF16),
            ],
            axis=1,
        )
        d_rows = dot_nt(both, gu_b[...]).astype(BF16).astype(F32)
        inverse = rsaved[micro_index][:, 0:1]
        gain = gain_b[...]
        scaled = [d_rows[:, q * wide : (q + 1) * wide] * gain_part(gain, q) for q in range(parts)]
        v = [vrows[micro_index, q * rows : (q + 1) * rows].astype(F32) for q in range(parts)]
        inner = jnp.zeros((rows, 1), F32)
        for q in range(parts):
            inner = inner + jnp.sum(scaled[q] * v[q], axis=1, keepdims=True)
        back = inner * (1.0 / width) * inverse * inverse * inverse
        finish(
            c,
            jnp.concatenate(
                [
                    (part(dy, q) + (scaled[q] * inverse - v[q] * back)).astype(BF16)
                    for q in range(parts)
                ],
                axis=0,
            ),
        )

    def relay(micro_index, direction):
        c = 2 * micro_index + direction
        wait_bytes(rin.at[c], rin_sem.at[c])

        @pl.when(has_next)
        def _():
            moved = dot(rmat[c], rin[c].reshape(total, wide))
            rout[c] = moved.astype(BF16).reshape(group, ROWS, wide)
            send_chunks(
                rout.at[c],
                ein.at[c],
                lambda peer: source_stage + 1,
                jnp.where(source_stage % NEAR == NEAR - 1, 0, 1),
                group,
                rout_sem.at[c],
                ein_sem.at[c],
            )

        rows_kept = dot(aexp[c], rin[c].reshape(total, wide)).astype(BF16)
        for q in range(parts):
            kept[c, :, q * wide : (q + 1) * wide] = rows_kept[q * tokens : (q + 1) * tokens]
        out = (out_f, out_b)[direction].at[0, micro_index]

        @pl.when(at_home)
        def _():
            pltpu.make_async_copy(kept.at[c], out, out_sem.at[c]).start()

        @pl.when(jnp.logical_not(at_home))
        def _():
            pltpu.make_async_remote_copy(
                src_ref=kept.at[c],
                dst_ref=out,
                send_sem=kept_sem.at[c],
                recv_sem=out_sem.at[c],
                device_id=(source_stage, me),
                device_id_type=MESH,
            ).start()

    wait_bytes(mrecv, m_sem)
    mflat[...] = mrecv[...].reshape(rows * micro, 128)
    for micro_index in range(micro):
        lanes = mflat[pl.ds(micro_index, rows, stride=micro), :]
        for direction in range(2):
            column = lanes[:, direction * 64 : direction * 64 + 1]
            shares[2 * micro_index + direction] = jnp.broadcast_to(column, (rows, 128))
    loads[3].wait()
    loads[4].wait()
    for micro_index in range(micro):
        prepare_backward(micro_index)

    wait_bytes(crecv, c_sem)
    for c in range(chains):
        aexp[c] = expanded(crecv[:, c : c + 1])

    @pl.when(has_next)
    def _():
        wait_bytes(cnext, cnext_sem)
        for c in range(chains):
            rmat[c] = dot_tn(expanded(cnext[:, c : c + 1]), aexp[c]).astype(BF16)

    for i in (0, 1, 2, 5):
        loads[i].wait()

    def experts(micro_index):
        expert_forward(micro_index)
        expert_backward(micro_index)

        @pl.when(jnp.logical_and(first, micro_index == 0))
        def _():
            deal(1)

    def relays(micro_index):
        relay(micro_index, 0)
        relay(micro_index, 1)

    def step(turn, carry):
        odd, late = turn % 2, turn // 2
        micro_index = jnp.where(at_home, late, odd)
        second = jnp.where(at_home, odd, late)
        is_relay = second == jnp.where(source_stage < stage, 0, 1)
        pl.when(is_relay)(lambda: relays(micro_index))
        pl.when(jnp.logical_not(is_relay))(lambda: experts(micro_index))
        return carry

    lax.fori_loop(0, 2 * micro, step, 0)

    for c in range(chains):
        wait_bytes((out_f if c % 2 == 0 else out_b).at[0, c // 2], out_sem.at[c])

    @pl.when(at_home)
    def _():
        for c in range(chains):
            wait_bytes(eout.at[c, pl.ds(0, group - 1)], eout_sem.at[c])

    @pl.when(jnp.logical_not(at_home))
    def _():
        wait_bytes(csend, csend_sem)
        for c in range(chains):
            wait_bytes(kept.at[c], kept_sem.at[c])
            wait_bytes(eout.at[c], eout_sem.at[c])

    @pl.when(stage > 0)
    def _():
        wait_bytes(csend, cnsend_sem)

    wait_bytes(msend.at[pl.ds(0, group - 1)], msend_sem)
    for micro_index in range(micro):
        wait_bytes(sdisp.at[micro_index, pl.ds(0, group - 1)], sdisp_sem.at[micro_index])

    @pl.when(first)
    def _():
        for c in range(chains):
            wait_bytes(disp.at[c, pl.ds(0, group - 1)], disp_sem.at[c])

    @pl.when(has_next)
    def _():
        for c in range(chains):
            wait_bytes(rout.at[c], rout_sem.at[c])


def solution(mesh):
    stages, group = mesh.shape["pipe"], mesh.shape["expert"]

    def local(
        entering,
        first_gain,
        first_gate,
        first_up,
        first_down,
        first_route,
        first_share,
        saved_inputs,
        cotangent,
        second_gain,
        second_gate,
        second_up,
        second_down,
        second_route,
        second_share,
    ):
        micro, tokens, width = entering.shape
        hidden_width = first_gate.shape[-1]
        cap = 2 * tokens // group
        parts = ROWS // cap
        wide = width // parts
        rows, total, chains = group * cap, group * ROWS, 2 * micro
        vmem = pl.BlockSpec(memory_space=pltpu.VMEM)
        anywhere = pl.BlockSpec(memory_space=pl.ANY)
        dma = pltpu.SemaphoreType.DMA
        chunks = lambda count: pltpu.VMEM((count, group, ROWS, wide), BF16)
        state = jax.ShapeDtypeStruct((1, micro, tokens, width), BF16)
        return pl.pallas_call(
            functools.partial(
                kernel, (stages, group, micro, tokens, width, hidden_width, cap)
            ),
            out_shape=(state, state),
            in_specs=[vmem] * 9 + [anywhere] * 6,
            out_specs=(vmem, vmem),
            scratch_shapes=[
                pltpu.VMEM((width, 2 * hidden_width), BF16),
                pltpu.VMEM((hidden_width, width), BF16),
                pltpu.VMEM((width, 2 * hidden_width), BF16),
                pltpu.VMEM((hidden_width, width), BF16),
                chunks(chains),
                chunks(chains),
                chunks(chains),
                chunks(chains),
                chunks(chains),
                chunks(micro),
                chunks(micro),
                pltpu.VMEM((group, cap * micro, 128), F32),
                pltpu.VMEM((group, cap * micro, 128), F32),
                pltpu.VMEM((rows * micro, 128), F32),
                pltpu.VMEM((chains, rows, 128), F32),
                pltpu.VMEM((tokens, 128), F32),
                pltpu.VMEM((tokens, 128), F32),
                pltpu.VMEM((tokens, 128), F32),
                pltpu.VMEM((total, total), BF16),
                pltpu.VMEM((total, total), BF16),
                pltpu.VMEM((chains, total, total), BF16),
                pltpu.VMEM((chains, parts * tokens, total), BF16),
                pltpu.VMEM((micro, total, wide), BF16),
                pltpu.VMEM((micro, rows, hidden_width), F32),
                pltpu.VMEM((micro, rows, hidden_width), F32),
                pltpu.VMEM((micro, rows, 128), F32),
                pltpu.VMEM((chains, tokens, width), BF16),
                dma((6,)),
                dma((chains,)),
                dma((chains,)),
                dma((micro,)),
                dma,
                dma,
                dma,
                dma((chains,)),
                dma((chains,)),
                dma((chains,)),
                dma((chains,)),
                dma((micro,)),
                dma,
                dma,
                dma,
                dma((chains,)),
            ],
            compiler_params=pltpu.CompilerParams(
                collective_id=0, has_side_effects=True, vmem_limit_bytes=48 * 1024 * 1024
            ),
        )(
            entering,
            cotangent,
            saved_inputs,
            first_gain,
            second_gain,
            first_route,
            second_route,
            first_share,
            second_share,
            first_gate,
            first_up,
            first_down,
            second_gate,
            second_up,
            second_down,
        )

    return jax.shard_map(
        local,
        mesh=mesh,
        in_specs=(
            P(None, "expert", None),
            P("pipe", None),
            P("pipe", "expert", None, None),
            P("pipe", "expert", None, None),
            P("pipe", "expert", None, None),
            P("pipe", None, "expert", None),
            P("pipe", None, "expert"),
            P("pipe", None, "expert", None),
            P(None, "expert", None),
            P("pipe", None),
            P("pipe", "expert", None, None),
            P("pipe", "expert", None, None),
            P("pipe", "expert", None, None),
            P("pipe", None, "expert", None),
            P("pipe", None, "expert"),
        ),
        out_specs=(P("pipe", None, "expert", None), P("pipe", None, "expert", None)),
        check_vma=False,
    )
```

```python
import functools

import jax
import jax.numpy as jnp
from jax import lax
from jax.experimental import pallas as pl
from jax.experimental.pallas import tpu as pltpu
from jax.sharding import PartitionSpec as P

EPSILON = 1e-06
MESH = pl.DeviceIdType.MESH
F32 = jnp.float32
VMEM = 60 * 1024 * 1024
BF16 = jnp.bfloat16
ROWS = 16
NEAR = 4


def shift_of(block):
    return jnp.where(block % 4 == 1, NEAR, 0) - jnp.where(block % 4 == 3, NEAR, 0)


def relay_of(stage, block, stages):
    return lax.rem(stage + shift_of(block) + stages, stages)


def relayed_by(place, block, stages):
    return lax.rem(place - shift_of(block) + stages, stages)


def iota(shape, dim):
    return lax.broadcasted_iota(jnp.int32, shape, dim)


def dot(a, b):
    return jnp.dot(a, b, preferred_element_type=F32)


def dot_nt(a, b):
    return lax.dot_general(a, b, (((1,), (1,)), ((), ())), preferred_element_type=F32)


def dot_tn(a, b):
    return lax.dot_general(a, b, (((0,), (0,)), ((), ())), preferred_element_type=F32)


def kernel(
    sizes,
    entering_hbm,
    cotangent_hbm,
    saved_hbm,
    gain_f_hbm,
    gain_b_hbm,
    route_f_hbm,
    route_b_hbm,
    share_f_hbm,
    share_b_hbm,
    gate_f,
    up_f,
    down_f,
    gate_b,
    up_b,
    down_b,
    out_f,
    out_b,
    entering,
    cotangent,
    saved,
    gain_f,
    gain_b,
    route_f,
    route_b,
    share_f,
    share_b,
    gu_f,
    dn_f,
    gu_b,
    dn_b,
    ein,
    eout,
    rin,
    rout,
    disp,
    sdisp,
    sin,
    msend,
    mrecv,
    mflat,
    shares,
    csend,
    crecv,
    cnext,
    perm,
    permt,
    rmat,
    aexp,
    vrows,
    fact1,
    fact2,
    rsaved,
    kept,
    w_sem,
    i_sem,
    ein_sem,
    rin_sem,
    sin_sem,
    m_sem,
    c_sem,
    cnext_sem,
    out_sem,
    eout_sem,
    rout_sem,
    disp_sem,
    sdisp_sem,
    msend_sem,
    csend_sem,
    cnsend_sem,
    kept_sem,
):
    stages, group, micro, tokens, width, hidden_width, cap = sizes
    parts = ROWS // cap
    wide = width // parts
    rows = group * cap
    total = group * ROWS
    chains = 2 * micro
    stage = lax.axis_index("pipe")
    me = lax.axis_index("expert")
    first = stage == 0
    host = relay_of(stage, me, stages)
    source_stage = relayed_by(stage, me, stages)
    has_next = source_stage < stages - 1
    at_home = host == stage

    weights = [
        (gate_f.at[0, 0], gu_f.at[:, 0:hidden_width]),
        (up_f.at[0, 0], gu_f.at[:, hidden_width : 2 * hidden_width]),
        (down_f.at[0, 0], dn_f),
        (gate_b.at[0, 0], gu_b.at[:, 0:hidden_width]),
        (up_b.at[0, 0], gu_b.at[:, hidden_width : 2 * hidden_width]),
        (down_b.at[0, 0], dn_b),
    ]
    loads = [pltpu.make_async_copy(s, d, w_sem.at[i]) for i, (s, d) in enumerate(weights)]
    inputs = [
        pltpu.make_async_copy(s, d, i_sem.at[i])
        for i, (s, d) in enumerate(
            [
                (route_f_hbm, route_f),
                (route_b_hbm, route_b),
                (entering_hbm, entering),
                (cotangent_hbm, cotangent),
                (share_f_hbm, share_f),
                (share_b_hbm, share_b),
                (saved_hbm, saved),
                (gain_f_hbm, gain_f),
                (gain_b_hbm, gain_b),
            ]
        )
    ]
    for load in inputs:
        load.start()
    for load in loads:
        load.start()

    barrier = pltpu.get_barrier_semaphore()

    def greet(pipe, peer):
        pl.semaphore_signal(barrier, inc=1, device_id=(pipe, peer), device_id_type=MESH)

    def greet_group(i, carry):
        greet(stage, lax.rem(me + i, group))
        return carry

    lax.fori_loop(1, group, greet_group, 0)

    @pl.when(jnp.logical_not(at_home))
    def _():
        def greet_source(i, carry):
            greet(source_stage, lax.rem(me + i, group))
            return carry

        lax.fori_loop(0, group, greet_source, 0)
        greet(host, me)

    @pl.when(stage > 0)
    def _():
        def greet_before(i, carry):
            peer = lax.rem(me + i, group)
            greet(relay_of(stage - 1, peer, stages), peer)
            return carry

        lax.fori_loop(0, group, greet_before, 0)

    @pl.when(has_next)
    def _():
        greet(source_stage + 1, me)

    def column_to_row(column):
        eye = iota((tokens, tokens), 0) == iota((tokens, tokens), 1)
        return jnp.sum(jnp.where(eye, column, 0.0), axis=0, keepdims=True)

    def row_to_column(row):
        eye = iota((tokens, tokens), 0) == iota((tokens, tokens), 1)
        return jnp.sum(jnp.where(eye, row, 0.0), axis=1, keepdims=True)

    def code_of(route_column):
        member = (iota((tokens, 128), 1).astype(F32) == route_column).astype(BF16)
        same = dot_nt(member, member)
        before = iota((tokens, tokens), 1) < iota((tokens, tokens), 0)
        slot = jnp.sum(jnp.where(before, same, 0.0), axis=1, keepdims=True)
        return route_column * ROWS + slot

    def expanded(code):
        column = jnp.concatenate([code + q * cap for q in range(parts)], axis=0)
        return (iota((parts * tokens, total), 1).astype(F32) == column).astype(BF16)

    inputs[0].wait()
    inputs[1].wait()
    codes = []
    for micro_index in range(micro):
        for route in (route_f, route_b):
            codes.append(code_of(row_to_column(route[micro_index].astype(F32))))
    def chunk_row(index):
        return lax.rem(index, rows) // cap * ROWS + index // rows * cap + lax.rem(index, cap)

    perm[...] = (iota((total, total), 1) == chunk_row(iota((total, total), 0))).astype(BF16)
    permt[...] = (iota((total, total), 0) == chunk_row(iota((total, total), 1))).astype(BF16)

    def stacked(values):
        return jnp.concatenate([values[:, q * wide : (q + 1) * wide] for q in range(parts)], axis=0)

    def scatter(table, values):
        return dot_tn(table, stacked(values)).astype(BF16).reshape(group, ROWS, wide)

    def send_chunks(source, target, pipe_of, far, count, send_sem, recv_sem):
        def send(i, carry):
            across, j = i // 8, i % 8 // 2
            step_x = jnp.where(j < 2, 2 + j, 3 - j)
            peer = (
                (me // 4 + step_x) % 4 * 4 + (me % 4 // 2 + far + across) % 2 * 2 + (me + 1 + i) % 2
            )
            pltpu.make_async_remote_copy(
                src_ref=source.at[peer],
                dst_ref=target.at[me],
                send_sem=send_sem,
                recv_sem=recv_sem,
                device_id=(pipe_of(peer), peer),
                device_id_type=MESH,
            ).start()
            return carry

        lax.fori_loop(0, count, send, 0, unroll=True)

    def send_group(source, target, send_sem, recv_sem):
        send_chunks(source, target, lambda peer: stage, 1, group - 1, send_sem, recv_sem)
        pltpu.make_async_copy(source.at[me], target.at[me], recv_sem).start()

    def wait_bytes(ref, sem):
        pltpu.make_async_copy(ref, ref, sem).wait()

    def place(micro_index):
        for c in (2 * micro_index, 2 * micro_index + 1):
            source = entering if c % 2 == 0 else cotangent
            disp[c] = scatter(expanded(codes[c]), source[micro_index])

    def deal(micro_index):
        for c in (2 * micro_index, 2 * micro_index + 1):
            send_group(disp.at[c], ein.at[c], disp_sem.at[c], ein_sem.at[c])

    def place_saved(micro_index):
        sdisp[micro_index] = scatter(
            expanded(codes[2 * micro_index + 1]), saved[0, micro_index]
        )

    def deal_saved(micro_index):
        send_group(
            sdisp.at[micro_index], sin.at[micro_index], sdisp_sem.at[micro_index], sin_sem.at[micro_index]
        )

    inputs[6].wait()
    place_saved(0)
    inputs[2].wait()
    inputs[3].wait()

    @pl.when(first)
    def _():
        place(0)

    inputs[4].wait()
    inputs[5].wait()

    for direction, share in ((0, share_f), (1, share_b)):
        column = jnp.zeros((rows * micro, 1), F32)
        for micro_index in range(micro):
            code_row = column_to_row(codes[2 * micro_index + direction])
            index = iota((rows * micro, tokens), 0)
            row_code = index // (cap * micro) * ROWS + lax.rem(index, cap * micro) // micro
            hit = jnp.logical_and(
                row_code.astype(F32) == code_row, lax.rem(index, micro) == micro_index
            )
            share_row = share[0, micro_index : micro_index + 1]
            column = column + jnp.sum(jnp.where(hit, share_row, 0.0), axis=1, keepdims=True)
        msend[:, :, direction * 64 : direction * 64 + 64] = jnp.broadcast_to(
            column, (rows * micro, 64)
        ).reshape(group, cap * micro, 64)

    lane = iota((tokens, 128), 1)
    packed = jnp.zeros((tokens, 128), F32)
    for c in range(chains):
        packed = packed + jnp.where(lane == c, codes[c], 0.0)
    csend[...] = packed

    greeted = (
        group - 1
        + group // 2
        + jnp.where(has_next, group, 0)
        + jnp.where(first, 0, 1)
        + jnp.where(at_home, 0, 1)
    )
    pl.semaphore_wait(barrier, greeted)

    @pl.when(first)
    def _():
        deal_saved(0)
        deal(0)

    send_group(msend, mrecv, msend_sem, m_sem)

    def code_copy(target, send_sem, recv_sem, pipe):
        return pltpu.make_async_remote_copy(
            src_ref=csend,
            dst_ref=target,
            send_sem=send_sem,
            recv_sem=recv_sem,
            device_id=(pipe, me),
            device_id_type=MESH,
        )

    @pl.when(at_home)
    def _():
        pltpu.make_async_copy(csend, crecv, c_sem).start()

    @pl.when(jnp.logical_not(at_home))
    def _():
        code_copy(crecv, csend_sem, c_sem, host).start()

    @pl.when(stage > 0)
    def _():
        code_copy(cnext, cnsend_sem, cnext_sem, relay_of(stage - 1, me, stages)).start()

    def arrange(chunks):
        return dot(perm[...], chunks.reshape(total, wide))

    def part(values, q):
        return values[q * rows : (q + 1) * rows]

    def gain_part(gain, q):
        return gain[:, q * wide : (q + 1) * wide]

    def row_sum(values, weigh):
        result = jnp.zeros((rows, 1), F32)
        for q in range(parts):
            result = result + jnp.sum(weigh(q, part(values, q)), axis=1, keepdims=True)
        return result

    def inverse_scale(values):
        squares = row_sum(values, lambda q, v: v * v) * (1.0 / width)
        return lax.rsqrt(squares + EPSILON)

    def normed(values, inverse, gain):
        return jnp.concatenate(
            [(part(values, q) * inverse * gain_part(gain, q)).astype(BF16) for q in range(parts)],
            axis=1,
        )

    def finish(c, values):
        eout[c] = dot(permt[...], values).astype(BF16).reshape(group, ROWS, wide)
        send_chunks(
            eout.at[c],
            rin.at[c],
            lambda peer: relay_of(stage, peer, stages),
            1,
            group - 1,
            eout_sem.at[c],
            rin_sem.at[c],
        )

        @pl.when(at_home)
        def _():
            pltpu.make_async_copy(eout.at[c, me], rin.at[c, me], rin_sem.at[c]).start()

        @pl.when(jnp.logical_not(at_home))
        def _():
            pltpu.make_async_remote_copy(
                src_ref=eout.at[c, me],
                dst_ref=rin.at[c, me],
                send_sem=eout_sem.at[c],
                recv_sem=rin_sem.at[c],
                device_id=(host, me),
                device_id_type=MESH,
            ).start()

    def expert_forward(micro_index):
        c = 2 * micro_index
        wait_bytes(ein.at[c], ein_sem.at[c])
        x = arrange(ein[c])
        gain = gain_f[...]
        pre = dot(normed(x, inverse_scale(x), gain), gu_f[...])
        pre_gate, pre_up = pre[:, :hidden_width], pre[:, hidden_width:]
        hidden = (pre_gate / (1.0 + jnp.exp(-pre_gate)) * pre_up).astype(BF16)
        out = dot(hidden, dn_f[...]).astype(BF16).astype(F32)
        share = shares[c][:, 0:1]
        finish(
            c,
            jnp.concatenate(
                [
                    (part(x, q) + share * out[:, q * wide : (q + 1) * wide]).astype(BF16)
                    for q in range(parts)
                ],
                axis=0,
            ),
        )

    def prepare_backward(micro_index):
        wait_bytes(sin.at[micro_index], sin_sem.at[micro_index])
        v = arrange(sin[micro_index])
        vrows[micro_index] = v.astype(BF16)
        inverse = inverse_scale(v)
        rsaved[micro_index] = jnp.broadcast_to(inverse, (rows, 128))
        back = dot(normed(v, inverse, gain_b[...]), gu_b[...])
        back_gate, back_up = back[:, :hidden_width], back[:, hidden_width:]
        s = 1.0 / (1.0 + jnp.exp(-back_gate))
        fact1[micro_index] = back_up * s * (1.0 + back_gate * (1.0 - s))
        fact2[micro_index] = back_gate * s

    def expert_backward(micro_index):
        c = 2 * micro_index + 1
        wait_bytes(ein.at[c], ein_sem.at[c])
        dy = arrange(ein[c])
        share = shares[c][:, 0:1]
        sent = jnp.concatenate(
            [(share * part(dy, q)).astype(BF16) for q in range(parts)], axis=1
        )
        d_hidden = dot_nt(sent, dn_b[...])
        both = jnp.concatenate(
            [
                (d_hidden * fact1[micro_index]).astype(BF16),
                (d_hidden * fact2[micro_index]).astype(BF16),
            ],
            axis=1,
        )
        d_rows = dot_nt(both, gu_b[...]).astype(BF16).astype(F32)
        inverse = rsaved[micro_index][:, 0:1]
        gain = gain_b[...]
        scaled = [d_rows[:, q * wide : (q + 1) * wide] * gain_part(gain, q) for q in range(parts)]
        v = [vrows[micro_index, q * rows : (q + 1) * rows].astype(F32) for q in range(parts)]
        inner = jnp.zeros((rows, 1), F32)
        for q in range(parts):
            inner = inner + jnp.sum(scaled[q] * v[q], axis=1, keepdims=True)
        back = inner * (1.0 / width) * inverse * inverse * inverse
        finish(
            c,
            jnp.concatenate(
                [
                    (part(dy, q) + (scaled[q] * inverse - v[q] * back)).astype(BF16)
                    for q in range(parts)
                ],
                axis=0,
            ),
        )

    def relay(micro_index, direction):
        c = 2 * micro_index + direction
        wait_bytes(rin.at[c], rin_sem.at[c])

        @pl.when(has_next)
        def _():
            moved = dot(rmat[c], rin[c].reshape(total, wide))
            rout[c] = moved.astype(BF16).reshape(group, ROWS, wide)
            send_chunks(
                rout.at[c],
                ein.at[c],
                lambda peer: source_stage + 1,
                jnp.where(source_stage % NEAR == NEAR - 1, 0, 1),
                group,
                rout_sem.at[c],
                ein_sem.at[c],
            )

        rows_kept = dot(aexp[c], rin[c].reshape(total, wide)).astype(BF16)
        for q in range(parts):
            kept[c, :, q * wide : (q + 1) * wide] = rows_kept[q * tokens : (q + 1) * tokens]
        out = (out_f, out_b)[direction].at[0, micro_index]

        @pl.when(at_home)
        def _():
            pltpu.make_async_copy(kept.at[c], out, out_sem.at[c]).start()

        @pl.when(jnp.logical_not(at_home))
        def _():
            pltpu.make_async_remote_copy(
                src_ref=kept.at[c],
                dst_ref=out,
                send_sem=kept_sem.at[c],
                recv_sem=out_sem.at[c],
                device_id=(source_stage, me),
                device_id_type=MESH,
            ).start()

    def prepare_relay():
        wait_bytes(crecv, c_sem)
        for c in range(chains):
            aexp[c] = expanded(crecv[:, c : c + 1])

        @pl.when(has_next)
        def _():
            wait_bytes(cnext, cnext_sem)
            for c in range(chains):
                rmat[c] = dot_tn(expanded(cnext[:, c : c + 1]), aexp[c]).astype(BF16)

    @pl.when(first)
    def _():
        place_saved(1)
        deal_saved(1)

    @pl.when(jnp.logical_not(first))
    def _():
        prepare_relay()
        deal_saved(0)
        place_saved(1)
        deal_saved(1)

    wait_bytes(mrecv, m_sem)
    mflat[...] = mrecv[...].reshape(rows * micro, 128)
    for micro_index in range(micro):
        lanes = mflat[pl.ds(micro_index, rows, stride=micro), :]
        for direction in range(2):
            column = lanes[:, direction * 64 : direction * 64 + 1]
            shares[2 * micro_index + direction] = jnp.broadcast_to(column, (rows, 128))
    for load in inputs[7:] + loads:
        load.wait()

    prepare_backward(0)

    @pl.when(jnp.logical_not(first))
    def _():
        prepare_backward(1)

    def experts(micro_index):
        expert_forward(micro_index)

        @pl.when(jnp.logical_and(first, micro_index == 0))
        def _():
            prepare_backward(1)

        expert_backward(micro_index)

        @pl.when(jnp.logical_and(first, micro_index == 0))
        def _():
            prepare_relay()
            place(1)
            deal(1)

    def relays(micro_index):
        relay(micro_index, 0)
        relay(micro_index, 1)

    def step(turn, carry):
        odd, late = turn % 2, turn // 2
        micro_index = jnp.where(at_home, late, odd)
        second = jnp.where(at_home, odd, late)
        is_relay = second == jnp.where(source_stage < stage, 0, 1)
        pl.when(is_relay)(lambda: relays(micro_index))
        pl.when(jnp.logical_not(is_relay))(lambda: experts(micro_index))
        return carry

    lax.fori_loop(0, 2 * micro, step, 0)

    for c in range(chains):
        wait_bytes((out_f if c % 2 == 0 else out_b).at[0, c // 2], out_sem.at[c])

    @pl.when(at_home)
    def _():
        for c in range(chains):
            wait_bytes(eout.at[c, pl.ds(0, group - 1)], eout_sem.at[c])

    @pl.when(jnp.logical_not(at_home))
    def _():
        wait_bytes(csend, csend_sem)
        for c in range(chains):
            wait_bytes(kept.at[c], kept_sem.at[c])
            wait_bytes(eout.at[c], eout_sem.at[c])

    @pl.when(stage > 0)
    def _():
        wait_bytes(csend, cnsend_sem)

    wait_bytes(msend.at[pl.ds(0, group - 1)], msend_sem)
    for micro_index in range(micro):
        wait_bytes(sdisp.at[micro_index, pl.ds(0, group - 1)], sdisp_sem.at[micro_index])

    @pl.when(first)
    def _():
        for c in range(chains):
            wait_bytes(disp.at[c, pl.ds(0, group - 1)], disp_sem.at[c])

    @pl.when(has_next)
    def _():
        for c in range(chains):
            wait_bytes(rout.at[c], rout_sem.at[c])


def solution(mesh):
    stages, group = mesh.shape["pipe"], mesh.shape["expert"]

    def local(
        entering,
        first_gain,
        first_gate,
        first_up,
        first_down,
        first_route,
        first_share,
        saved_inputs,
        cotangent,
        second_gain,
        second_gate,
        second_up,
        second_down,
        second_route,
        second_share,
    ):
        micro, tokens, width = entering.shape
        hidden_width = first_gate.shape[-1]
        cap = 2 * tokens // group
        parts = ROWS // cap
        wide = width // parts
        rows, total, chains = group * cap, group * ROWS, 2 * micro
        vmem = pl.BlockSpec(memory_space=pltpu.VMEM)
        anywhere = pl.BlockSpec(memory_space=pl.ANY)
        dma = pltpu.SemaphoreType.DMA
        chunks = lambda count: pltpu.VMEM((count, group, ROWS, wide), BF16)
        state = jax.ShapeDtypeStruct((1, micro, tokens, width), BF16)
        return pl.pallas_call(
            functools.partial(
                kernel, (stages, group, micro, tokens, width, hidden_width, cap)
            ),
            out_shape=(state, state),
            in_specs=[anywhere] * 15,
            out_specs=(vmem, vmem),
            scratch_shapes=[
                pltpu.VMEM((micro, tokens, width), BF16),
                pltpu.VMEM((micro, tokens, width), BF16),
                pltpu.VMEM((1, micro, tokens, width), BF16),
                pltpu.VMEM((1, width), F32),
                pltpu.VMEM((1, width), F32),
                pltpu.VMEM((micro, 1, tokens), jnp.int32),
                pltpu.VMEM((micro, 1, tokens), jnp.int32),
                pltpu.VMEM((1, micro, tokens), F32),
                pltpu.VMEM((1, micro, tokens), F32),
                pltpu.VMEM((width, 2 * hidden_width), BF16),
                pltpu.VMEM((hidden_width, width), BF16),
                pltpu.VMEM((width, 2 * hidden_width), BF16),
                pltpu.VMEM((hidden_width, width), BF16),
                chunks(chains),
                chunks(chains),
                chunks(chains),
                chunks(chains),
                chunks(chains),
                chunks(micro),
                chunks(micro),
                pltpu.VMEM((group, cap * micro, 128), F32),
                pltpu.VMEM((group, cap * micro, 128), F32),
                pltpu.VMEM((rows * micro, 128), F32),
                pltpu.VMEM((chains, rows, 128), F32),
                pltpu.VMEM((tokens, 128), F32),
                pltpu.VMEM((tokens, 128), F32),
                pltpu.VMEM((tokens, 128), F32),
                pltpu.VMEM((total, total), BF16),
                pltpu.VMEM((total, total), BF16),
                pltpu.VMEM((chains, total, total), BF16),
                pltpu.VMEM((chains, parts * tokens, total), BF16),
                pltpu.VMEM((micro, total, wide), BF16),
                pltpu.VMEM((micro, rows, hidden_width), F32),
                pltpu.VMEM((micro, rows, hidden_width), F32),
                pltpu.VMEM((micro, rows, 128), F32),
                pltpu.VMEM((chains, tokens, width), BF16),
                dma((6,)),
                dma((9,)),
                dma((chains,)),
                dma((chains,)),
                dma((micro,)),
                dma,
                dma,
                dma,
                dma((chains,)),
                dma((chains,)),
                dma((chains,)),
                dma((chains,)),
                dma((micro,)),
                dma,
                dma,
                dma,
                dma((chains,)),
            ],
            compiler_params=pltpu.CompilerParams(
                collective_id=0, has_side_effects=True, vmem_limit_bytes=VMEM
            ),
        )(
            entering,
            cotangent,
            saved_inputs,
            first_gain,
            second_gain,
            first_route.reshape(micro, 1, tokens),
            second_route.reshape(micro, 1, tokens),
            first_share,
            second_share,
            first_gate,
            first_up,
            first_down,
            second_gate,
            second_up,
            second_down,
        )

    return jax.shard_map(
        local,
        mesh=mesh,
        in_specs=(
            P(None, "expert", None),
            P("pipe", None),
            P("pipe", "expert", None, None),
            P("pipe", "expert", None, None),
            P("pipe", "expert", None, None),
            P("pipe", None, "expert", None),
            P("pipe", None, "expert"),
            P("pipe", None, "expert", None),
            P(None, "expert", None),
            P("pipe", None),
            P("pipe", "expert", None, None),
            P("pipe", "expert", None, None),
            P("pipe", "expert", None, None),
            P("pipe", None, "expert", None),
            P("pipe", None, "expert"),
        ),
        out_specs=(P("pipe", None, "expert", None), P("pipe", None, "expert", None)),
        check_vma=False,
    )
```

```python
import functools

import jax
import jax.numpy as jnp
from jax import lax
from jax.experimental import pallas as pl
from jax.experimental.pallas import tpu as pltpu
from jax.sharding import PartitionSpec as P

EPSILON = 1e-06
MESH = pl.DeviceIdType.MESH
F32 = jnp.float32
VMEM = 60 * 1024 * 1024
BF16 = jnp.bfloat16
ROWS = 16
NEAR = 4


def shift_of(block):
    return jnp.where(block % 4 == 1, NEAR, 0) - jnp.where(block % 4 == 3, NEAR, 0)


def relay_of(stage, block, stages):
    return lax.rem(stage + shift_of(block) + stages, stages)


def relayed_by(place, block, stages):
    return lax.rem(place - shift_of(block) + stages, stages)


def iota(shape, dim):
    return lax.broadcasted_iota(jnp.int32, shape, dim)


def dot(a, b):
    return jnp.dot(a, b, preferred_element_type=F32)


def dot_nt(a, b):
    return lax.dot_general(a, b, (((1,), (1,)), ((), ())), preferred_element_type=F32)


def dot_tn(a, b):
    return lax.dot_general(a, b, (((0,), (0,)), ((), ())), preferred_element_type=F32)


def kernel(
    sizes,
    entering_hbm,
    cotangent_hbm,
    saved_hbm,
    gain_f_hbm,
    gain_b_hbm,
    route_f_hbm,
    route_b_hbm,
    share_f_hbm,
    share_b_hbm,
    gate_f,
    up_f,
    down_f,
    gate_b,
    up_b,
    down_b,
    out_f,
    out_b,
    entering,
    cotangent,
    saved,
    gain_f,
    gain_b,
    route_f,
    route_b,
    share_f,
    share_b,
    gu_f,
    dn_f,
    gu_b,
    dn_b,
    ein,
    eout,
    rin,
    rout,
    disp,
    sdisp,
    sin,
    msend,
    mrecv,
    mflat,
    shares,
    csend,
    crecv,
    cnext,
    perm,
    permt,
    rmat,
    aexp,
    vrows,
    fact1,
    fact2,
    rsaved,
    kept,
    w_sem,
    i_sem,
    ein_sem,
    rin_sem,
    sin_sem,
    m_sem,
    c_sem,
    cnext_sem,
    out_sem,
    eout_sem,
    rout_sem,
    disp_sem,
    sdisp_sem,
    msend_sem,
    csend_sem,
    cnsend_sem,
    kept_sem,
):
    stages, group, micro, tokens, width, hidden_width, cap = sizes
    parts = ROWS // cap
    wide = width // parts
    rows = group * cap
    total = group * ROWS
    chains = 2 * micro
    stage = lax.axis_index("pipe")
    me = lax.axis_index("expert")
    first = stage == 0
    host = relay_of(stage, me, stages)
    source_stage = relayed_by(stage, me, stages)
    has_next = source_stage < stages - 1
    at_home = host == stage

    weights = [
        (gate_f.at[0, 0], gu_f.at[:, 0:hidden_width]),
        (up_f.at[0, 0], gu_f.at[:, hidden_width : 2 * hidden_width]),
        (down_f.at[0, 0], dn_f),
        (gate_b.at[0, 0], gu_b.at[:, 0:hidden_width]),
        (up_b.at[0, 0], gu_b.at[:, hidden_width : 2 * hidden_width]),
        (down_b.at[0, 0], dn_b),
    ]
    loads = [pltpu.make_async_copy(s, d, w_sem.at[i]) for i, (s, d) in enumerate(weights)]
    inputs = [
        pltpu.make_async_copy(s, d, i_sem.at[i])
        for i, (s, d) in enumerate(
            [
                (route_f_hbm, route_f),
                (route_b_hbm, route_b),
                (entering_hbm, entering),
                (cotangent_hbm, cotangent),
                (share_f_hbm, share_f),
                (share_b_hbm, share_b),
                (saved_hbm, saved),
                (gain_f_hbm, gain_f),
                (gain_b_hbm, gain_b),
            ]
        )
    ]
    for load in inputs:
        load.start()
    for load in loads:
        load.start()

    barrier = pltpu.get_barrier_semaphore()

    def greet(pipe, peer):
        pl.semaphore_signal(barrier, inc=1, device_id=(pipe, peer), device_id_type=MESH)

    def greet_group(i, carry):
        greet(stage, lax.rem(me + i, group))
        return carry

    lax.fori_loop(1, group, greet_group, 0)

    @pl.when(jnp.logical_not(at_home))
    def _():
        def greet_source(i, carry):
            greet(source_stage, lax.rem(me + i, group))
            return carry

        lax.fori_loop(0, group, greet_source, 0)
        greet(host, me)

    @pl.when(stage > 0)
    def _():
        def greet_before(i, carry):
            peer = lax.rem(me + i, group)
            greet(relay_of(stage - 1, peer, stages), peer)
            return carry

        lax.fori_loop(0, group, greet_before, 0)

    @pl.when(has_next)
    def _():
        greet(source_stage + 1, me)

    def column_to_row(column):
        eye = iota((tokens, tokens), 0) == iota((tokens, tokens), 1)
        return jnp.sum(jnp.where(eye, column, 0.0), axis=0, keepdims=True)

    def row_to_column(row):
        eye = iota((tokens, tokens), 0) == iota((tokens, tokens), 1)
        return jnp.sum(jnp.where(eye, row, 0.0), axis=1, keepdims=True)

    def code_of(route_column):
        member = (iota((tokens, 128), 1).astype(F32) == route_column).astype(BF16)
        same = dot_nt(member, member)
        before = iota((tokens, tokens), 1) < iota((tokens, tokens), 0)
        slot = jnp.sum(jnp.where(before, same, 0.0), axis=1, keepdims=True)
        return route_column * ROWS + slot

    def expanded(code):
        column = jnp.concatenate([code + q * cap for q in range(parts)], axis=0)
        return (iota((parts * tokens, total), 1).astype(F32) == column).astype(BF16)

    inputs[0].wait()
    inputs[1].wait()
    codes = []
    for micro_index in range(micro):
        for route in (route_f, route_b):
            codes.append(code_of(row_to_column(route[micro_index].astype(F32))))
    def chunk_row(index):
        return lax.rem(index, rows) // cap * ROWS + index // rows * cap + lax.rem(index, cap)

    perm[...] = (iota((total, total), 1) == chunk_row(iota((total, total), 0))).astype(BF16)
    permt[...] = (iota((total, total), 0) == chunk_row(iota((total, total), 1))).astype(BF16)

    def stacked(values):
        return jnp.concatenate([values[:, q * wide : (q + 1) * wide] for q in range(parts)], axis=0)

    def scatter(table, values):
        return dot_tn(table, stacked(values)).astype(BF16).reshape(group, ROWS, wide)

    def send_chunks(source, target, pipe_of, far, count, send_sem, recv_sem):
        def send(i, carry):
            across, j = i // 8, i % 8 // 2
            step_x = jnp.where(j < 2, 2 + j, 3 - j)
            peer = (
                (me // 4 + step_x) % 4 * 4 + (me % 4 // 2 + far + across) % 2 * 2 + (me + 1 + i) % 2
            )
            pltpu.make_async_remote_copy(
                src_ref=source.at[peer],
                dst_ref=target.at[me],
                send_sem=send_sem,
                recv_sem=recv_sem,
                device_id=(pipe_of(peer), peer),
                device_id_type=MESH,
            ).start()
            return carry

        lax.fori_loop(0, count, send, 0, unroll=True)

    def send_group(source, target, send_sem, recv_sem):
        send_chunks(source, target, lambda peer: stage, 1, group - 1, send_sem, recv_sem)
        pltpu.make_async_copy(source.at[me], target.at[me], recv_sem).start()

    def wait_bytes(ref, sem):
        pltpu.make_async_copy(ref, ref, sem).wait()

    def place(micro_index):
        for c in (2 * micro_index, 2 * micro_index + 1):
            source = entering if c % 2 == 0 else cotangent
            disp[c] = scatter(expanded(codes[c]), source[micro_index])

    def deal(micro_index):
        for c in (2 * micro_index, 2 * micro_index + 1):
            send_group(disp.at[c], ein.at[c], disp_sem.at[c], ein_sem.at[c])

    def place_saved(micro_index):
        sdisp[micro_index] = scatter(
            expanded(codes[2 * micro_index + 1]), saved[0, micro_index]
        )

    def deal_saved(micro_index):
        send_group(
            sdisp.at[micro_index], sin.at[micro_index], sdisp_sem.at[micro_index], sin_sem.at[micro_index]
        )

    inputs[6].wait()
    place_saved(0)
    inputs[2].wait()
    inputs[3].wait()

    @pl.when(first)
    def _():
        place(0)

    inputs[4].wait()
    inputs[5].wait()

    for direction, share in ((0, share_f), (1, share_b)):
        column = jnp.zeros((rows * micro, 1), F32)
        for micro_index in range(micro):
            code_row = column_to_row(codes[2 * micro_index + direction])
            index = iota((rows * micro, tokens), 0)
            row_code = index // (cap * micro) * ROWS + lax.rem(index, cap * micro) // micro
            hit = jnp.logical_and(
                row_code.astype(F32) == code_row, lax.rem(index, micro) == micro_index
            )
            share_row = share[0, micro_index : micro_index + 1]
            column = column + jnp.sum(jnp.where(hit, share_row, 0.0), axis=1, keepdims=True)
        msend[:, :, direction * 64 : direction * 64 + 64] = jnp.broadcast_to(
            column, (rows * micro, 64)
        ).reshape(group, cap * micro, 64)

    lane = iota((tokens, 128), 1)
    packed = jnp.zeros((tokens, 128), F32)
    for c in range(chains):
        packed = packed + jnp.where(lane == c, codes[c], 0.0)
    csend[...] = packed

    greeted = (
        group - 1
        + group // 2
        + jnp.where(has_next, group, 0)
        + jnp.where(first, 0, 1)
        + jnp.where(at_home, 0, 1)
    )
    pl.semaphore_wait(barrier, greeted)

    @pl.when(first)
    def _():
        deal_saved(0)
        deal(0)

    send_group(msend, mrecv, msend_sem, m_sem)

    def code_copy(target, send_sem, recv_sem, pipe):
        return pltpu.make_async_remote_copy(
            src_ref=csend,
            dst_ref=target,
            send_sem=send_sem,
            recv_sem=recv_sem,
            device_id=(pipe, me),
            device_id_type=MESH,
        )

    @pl.when(at_home)
    def _():
        pltpu.make_async_copy(csend, crecv, c_sem).start()

    @pl.when(jnp.logical_not(at_home))
    def _():
        code_copy(crecv, csend_sem, c_sem, host).start()

    @pl.when(stage > 0)
    def _():
        code_copy(cnext, cnsend_sem, cnext_sem, relay_of(stage - 1, me, stages)).start()

    def arrange(chunks):
        return dot(perm[...], chunks.reshape(total, wide))

    def part(values, q):
        return values[q * rows : (q + 1) * rows]

    def gain_part(gain, q):
        return gain[:, q * wide : (q + 1) * wide]

    def row_sum(values, weigh):
        result = jnp.zeros((rows, 1), F32)
        for q in range(parts):
            result = result + jnp.sum(weigh(q, part(values, q)), axis=1, keepdims=True)
        return result

    def inverse_scale(values):
        squares = row_sum(values, lambda q, v: v * v) * (1.0 / width)
        return lax.rsqrt(squares + EPSILON)

    def normed(values, inverse, gain):
        return jnp.concatenate(
            [(part(values, q) * inverse * gain_part(gain, q)).astype(BF16) for q in range(parts)],
            axis=1,
        )

    def finish(c, values):
        eout[c] = dot(permt[...], values).astype(BF16).reshape(group, ROWS, wide)
        send_chunks(
            eout.at[c],
            rin.at[c],
            lambda peer: relay_of(stage, peer, stages),
            1,
            group - 1,
            eout_sem.at[c],
            rin_sem.at[c],
        )

        @pl.when(at_home)
        def _():
            pltpu.make_async_copy(eout.at[c, me], rin.at[c, me], rin_sem.at[c]).start()

        @pl.when(jnp.logical_not(at_home))
        def _():
            pltpu.make_async_remote_copy(
                src_ref=eout.at[c, me],
                dst_ref=rin.at[c, me],
                send_sem=eout_sem.at[c],
                recv_sem=rin_sem.at[c],
                device_id=(host, me),
                device_id_type=MESH,
            ).start()

    def expert_forward(micro_index):
        c = 2 * micro_index
        wait_bytes(ein.at[c], ein_sem.at[c])
        x = arrange(ein[c])
        gain = gain_f[...]
        pre = dot(normed(x, inverse_scale(x), gain), gu_f[...])
        pre_gate, pre_up = pre[:, :hidden_width], pre[:, hidden_width:]
        hidden = (pre_gate / (1.0 + jnp.exp(-pre_gate)) * pre_up).astype(BF16)
        out = dot(hidden, dn_f[...]).astype(BF16).astype(F32)
        share = shares[c][:, 0:1]
        finish(
            c,
            jnp.concatenate(
                [
                    (part(x, q) + share * out[:, q * wide : (q + 1) * wide]).astype(BF16)
                    for q in range(parts)
                ],
                axis=0,
            ),
        )

    def prepare_backward(micro_index):
        wait_bytes(sin.at[micro_index], sin_sem.at[micro_index])
        v = arrange(sin[micro_index])
        vrows[micro_index] = v.astype(BF16)
        inverse = inverse_scale(v)
        rsaved[micro_index] = jnp.broadcast_to(inverse, (rows, 128))
        back = dot(normed(v, inverse, gain_b[...]), gu_b[...])
        back_gate, back_up = back[:, :hidden_width], back[:, hidden_width:]
        s = 1.0 / (1.0 + jnp.exp(-back_gate))
        fact1[micro_index] = back_up * s * (1.0 + back_gate * (1.0 - s))
        fact2[micro_index] = back_gate * s

    def expert_backward(micro_index):
        c = 2 * micro_index + 1
        wait_bytes(ein.at[c], ein_sem.at[c])
        dy = arrange(ein[c])
        share = shares[c][:, 0:1]
        sent = jnp.concatenate(
            [(share * part(dy, q)).astype(BF16) for q in range(parts)], axis=1
        )
        d_hidden = dot_nt(sent, dn_b[...])
        both = jnp.concatenate(
            [
                (d_hidden * fact1[micro_index]).astype(BF16),
                (d_hidden * fact2[micro_index]).astype(BF16),
            ],
            axis=1,
        )
        d_rows = dot_nt(both, gu_b[...]).astype(BF16).astype(F32)
        inverse = rsaved[micro_index][:, 0:1]
        gain = gain_b[...]
        scaled = [d_rows[:, q * wide : (q + 1) * wide] * gain_part(gain, q) for q in range(parts)]
        v = [vrows[micro_index, q * rows : (q + 1) * rows].astype(F32) for q in range(parts)]
        inner = jnp.zeros((rows, 1), F32)
        for q in range(parts):
            inner = inner + jnp.sum(scaled[q] * v[q], axis=1, keepdims=True)
        back = inner * (1.0 / width) * inverse * inverse * inverse
        finish(
            c,
            jnp.concatenate(
                [
                    (part(dy, q) + (scaled[q] * inverse - v[q] * back)).astype(BF16)
                    for q in range(parts)
                ],
                axis=0,
            ),
        )

    def relay(micro_index, direction):
        c = 2 * micro_index + direction
        wait_bytes(rin.at[c], rin_sem.at[c])

        @pl.when(has_next)
        def _():
            moved = dot(rmat[c], rin[c].reshape(total, wide))
            rout[c] = moved.astype(BF16).reshape(group, ROWS, wide)
            send_chunks(
                rout.at[c],
                ein.at[c],
                lambda peer: source_stage + 1,
                jnp.where(source_stage % NEAR == NEAR - 1, 0, 1),
                group,
                rout_sem.at[c],
                ein_sem.at[c],
            )

    def keep(micro_index, direction):
        c = 2 * micro_index + direction
        rows_kept = dot(aexp[c], rin[c].reshape(total, wide)).astype(BF16)
        for q in range(parts):
            kept[c, :, q * wide : (q + 1) * wide] = rows_kept[q * tokens : (q + 1) * tokens]
        out = (out_f, out_b)[direction].at[0, micro_index]

        @pl.when(at_home)
        def _():
            pltpu.make_async_copy(kept.at[c], out, out_sem.at[c]).start()

        @pl.when(jnp.logical_not(at_home))
        def _():
            pltpu.make_async_remote_copy(
                src_ref=kept.at[c],
                dst_ref=out,
                send_sem=kept_sem.at[c],
                recv_sem=out_sem.at[c],
                device_id=(source_stage, me),
                device_id_type=MESH,
            ).start()

    def prepare_relay():
        wait_bytes(crecv, c_sem)
        for c in range(chains):
            aexp[c] = expanded(crecv[:, c : c + 1])

        @pl.when(has_next)
        def _():
            wait_bytes(cnext, cnext_sem)
            for c in range(chains):
                rmat[c] = dot_tn(expanded(cnext[:, c : c + 1]), aexp[c]).astype(BF16)

    @pl.when(first)
    def _():
        place_saved(1)
        deal_saved(1)

    @pl.when(jnp.logical_not(first))
    def _():
        prepare_relay()
        deal_saved(0)
        place_saved(1)
        deal_saved(1)

    wait_bytes(mrecv, m_sem)
    mflat[...] = mrecv[...].reshape(rows * micro, 128)
    for micro_index in range(micro):
        lanes = mflat[pl.ds(micro_index, rows, stride=micro), :]
        for direction in range(2):
            column = lanes[:, direction * 64 : direction * 64 + 1]
            shares[2 * micro_index + direction] = jnp.broadcast_to(column, (rows, 128))
    for load in inputs[7:] + loads:
        load.wait()

    prepare_backward(0)

    @pl.when(jnp.logical_not(first))
    def _():
        prepare_backward(1)

    def experts(micro_index):
        expert_forward(micro_index)

        @pl.when(jnp.logical_and(first, micro_index == 0))
        def _():
            prepare_backward(1)

        expert_backward(micro_index)

        @pl.when(jnp.logical_and(first, micro_index == 0))
        def _():
            prepare_relay()
            place(1)
            deal(1)

    def relays(micro_index):
        relay(micro_index, 0)
        relay(micro_index, 1)
        keep(micro_index, 0)
        keep(micro_index, 1)

    def step(turn, carry):
        odd, late = turn % 2, turn // 2
        micro_index = jnp.where(at_home, late, odd)
        second = jnp.where(at_home, odd, late)
        is_relay = second == jnp.where(source_stage < stage, 0, 1)
        pl.when(is_relay)(lambda: relays(micro_index))
        pl.when(jnp.logical_not(is_relay))(lambda: experts(micro_index))
        return carry

    lax.fori_loop(0, 2 * micro, step, 0)

    for c in range(chains):
        wait_bytes((out_f if c % 2 == 0 else out_b).at[0, c // 2], out_sem.at[c])

    @pl.when(at_home)
    def _():
        for c in range(chains):
            wait_bytes(eout.at[c, pl.ds(0, group - 1)], eout_sem.at[c])

    @pl.when(jnp.logical_not(at_home))
    def _():
        wait_bytes(csend, csend_sem)
        for c in range(chains):
            wait_bytes(kept.at[c], kept_sem.at[c])
            wait_bytes(eout.at[c], eout_sem.at[c])

    @pl.when(stage > 0)
    def _():
        wait_bytes(csend, cnsend_sem)

    wait_bytes(msend.at[pl.ds(0, group - 1)], msend_sem)
    for micro_index in range(micro):
        wait_bytes(sdisp.at[micro_index, pl.ds(0, group - 1)], sdisp_sem.at[micro_index])

    @pl.when(first)
    def _():
        for c in range(chains):
            wait_bytes(disp.at[c, pl.ds(0, group - 1)], disp_sem.at[c])

    @pl.when(has_next)
    def _():
        for c in range(chains):
            wait_bytes(rout.at[c], rout_sem.at[c])


def solution(mesh):
    stages, group = mesh.shape["pipe"], mesh.shape["expert"]

    def local(
        entering,
        first_gain,
        first_gate,
        first_up,
        first_down,
        first_route,
        first_share,
        saved_inputs,
        cotangent,
        second_gain,
        second_gate,
        second_up,
        second_down,
        second_route,
        second_share,
    ):
        micro, tokens, width = entering.shape
        hidden_width = first_gate.shape[-1]
        cap = 2 * tokens // group
        parts = ROWS // cap
        wide = width // parts
        rows, total, chains = group * cap, group * ROWS, 2 * micro
        vmem = pl.BlockSpec(memory_space=pltpu.VMEM)
        anywhere = pl.BlockSpec(memory_space=pl.ANY)
        dma = pltpu.SemaphoreType.DMA
        chunks = lambda count: pltpu.VMEM((count, group, ROWS, wide), BF16)
        state = jax.ShapeDtypeStruct((1, micro, tokens, width), BF16)
        return pl.pallas_call(
            functools.partial(
                kernel, (stages, group, micro, tokens, width, hidden_width, cap)
            ),
            out_shape=(state, state),
            in_specs=[anywhere] * 15,
            out_specs=(vmem, vmem),
            scratch_shapes=[
                pltpu.VMEM((micro, tokens, width), BF16),
                pltpu.VMEM((micro, tokens, width), BF16),
                pltpu.VMEM((1, micro, tokens, width), BF16),
                pltpu.VMEM((1, width), F32),
                pltpu.VMEM((1, width), F32),
                pltpu.VMEM((micro, 1, tokens), jnp.int32),
                pltpu.VMEM((micro, 1, tokens), jnp.int32),
                pltpu.VMEM((1, micro, tokens), F32),
                pltpu.VMEM((1, micro, tokens), F32),
                pltpu.VMEM((width, 2 * hidden_width), BF16),
                pltpu.VMEM((hidden_width, width), BF16),
                pltpu.VMEM((width, 2 * hidden_width), BF16),
                pltpu.VMEM((hidden_width, width), BF16),
                chunks(chains),
                chunks(chains),
                chunks(chains),
                chunks(chains),
                chunks(chains),
                chunks(micro),
                chunks(micro),
                pltpu.VMEM((group, cap * micro, 128), F32),
                pltpu.VMEM((group, cap * micro, 128), F32),
                pltpu.VMEM((rows * micro, 128), F32),
                pltpu.VMEM((chains, rows, 128), F32),
                pltpu.VMEM((tokens, 128), F32),
                pltpu.VMEM((tokens, 128), F32),
                pltpu.VMEM((tokens, 128), F32),
                pltpu.VMEM((total, total), BF16),
                pltpu.VMEM((total, total), BF16),
                pltpu.VMEM((chains, total, total), BF16),
                pltpu.VMEM((chains, parts * tokens, total), BF16),
                pltpu.VMEM((micro, total, wide), BF16),
                pltpu.VMEM((micro, rows, hidden_width), F32),
                pltpu.VMEM((micro, rows, hidden_width), F32),
                pltpu.VMEM((micro, rows, 128), F32),
                pltpu.VMEM((chains, tokens, width), BF16),
                dma((6,)),
                dma((9,)),
                dma((chains,)),
                dma((chains,)),
                dma((micro,)),
                dma,
                dma,
                dma,
                dma((chains,)),
                dma((chains,)),
                dma((chains,)),
                dma((chains,)),
                dma((micro,)),
                dma,
                dma,
                dma,
                dma((chains,)),
            ],
            compiler_params=pltpu.CompilerParams(
                collective_id=0, has_side_effects=True, vmem_limit_bytes=VMEM
            ),
        )(
            entering,
            cotangent,
            saved_inputs,
            first_gain,
            second_gain,
            first_route.reshape(micro, 1, tokens),
            second_route.reshape(micro, 1, tokens),
            first_share,
            second_share,
            first_gate,
            first_up,
            first_down,
            second_gate,
            second_up,
            second_down,
        )

    return jax.shard_map(
        local,
        mesh=mesh,
        in_specs=(
            P(None, "expert", None),
            P("pipe", None),
            P("pipe", "expert", None, None),
            P("pipe", "expert", None, None),
            P("pipe", "expert", None, None),
            P("pipe", None, "expert", None),
            P("pipe", None, "expert"),
            P("pipe", None, "expert", None),
            P(None, "expert", None),
            P("pipe", None),
            P("pipe", "expert", None, None),
            P("pipe", "expert", None, None),
            P("pipe", "expert", None, None),
            P("pipe", None, "expert", None),
            P("pipe", None, "expert"),
        ),
        out_specs=(P("pipe", None, "expert", None), P("pipe", None, "expert", None)),
        check_vma=False,
    )
```
